32 devices in a mesh: gossip: 16 (over z, y, core), shard: 2 (over x).
Axes of the slice: x: 2, y: 2, z: 4, core: 2. Of those that a mesh axis runs over, the one named last changes fastest.
Arguments:
- feature_pool: bfloat16 [16, 2, 32, 32, 1408], P('gossip', None, 'shard'), may hold values from -6 to 6
- sample_ids: int32 [16], P('gossip'), may hold values from 0 to 1
- token_mask: int32 [16, 32, 32], P('gossip', 'shard'), may hold values 0 or 1
- step_index: int32 [1], replicated, may hold values from 0 to 1199
- dw_kernel: float32 [7, 7, 1408], replicated, may hold values from -0.875 to 0.875
- dw_bias: float32 [1408], replicated, may hold values from -3 to 3
- ln_gain: float32 [1408], replicated, may hold values from 0.1 to 1.9
- ln_bias: float32 [1408], replicated, may hold values from -3 to 3
- w_in: bfloat16 [16, 3072, 1408], P('gossip', 'shard'), may hold values from -0.5330018 to 0.5330018
- grn_gamma: float32 [16, 3072], P('gossip', 'shard'), may hold values from -3 to 3
- grn_beta: float32 [16, 3072], P('gossip', 'shard'), may hold values from -3 to 3
- w_out: bfloat16 [16, 3072, 1408], P('gossip', 'shard'), may hold values from -0.109375 to 0.109375
Outputs:
- grad_in: bfloat16 [16, 3072, 1408], P('gossip', 'shard')
- grad_out: bfloat16 [16, 3072, 1408], P('gossip', 'shard')
- grad_gamma: float32 [16, 3072], P('gossip', 'shard')
- grad_beta: float32 [16, 3072], P('gossip', 'shard')
The draws below stay inside these ranges and needn't reach their ends.
All inputs are finite; a program needn't handle non-finite values. No bound on the sum of `token_mask` on one device may be relied on, other than what follows from the above.
Results may differ from the reference program's by a relative error of at most 0.007.
Values may be sent and summed in bfloat16 or wider, within the bound.
No kernel may reach another device: no remote copies, remote signals or barrier semaphores. Data moves between devices by JAX's collectives and lax.ppermute only.
A program may use at most 128 MiB of HBM per device.

```python
import math
import jax
import jax.numpy as jnp
from jax import lax

C = 1408
HID = 3072
H = 32
W = 32
POOL = 2
N_GOSSIP = 16
N_SHARD = 2


def draw_w_in(key, part):
    key = jax.random.fold_in(key, 11)
    first, second = jax.random.split(key)
    base = jnp.clip(jax.random.normal(first, (N_GOSSIP, HID, C), jnp.float32), -5.0, 5.0)
    rise = jnp.exp(math.log(3.0) * jnp.arange(HID, dtype=jnp.float32) / HID)
    rough = jnp.exp(jax.random.uniform(second, (N_GOSSIP, HID, 1), jnp.float32, 0.0, math.log(4.0)))
    return (base * rise[None, :, None] * rough / (3.0 * math.sqrt(C))).astype(jnp.bfloat16)


def plant(drawn, rng, low, largest):
    dims = drawn.shape
    place = [jax.random.randint(jax.random.fold_in(rng, axis), (), 0, dims[axis]) for axis in range(len(dims))]
    drawn = drawn.at[tuple(place)].set(low)
    longest = dims.index(max(dims))
    place[longest] = (place[longest] + 1) % dims[longest]
    return drawn.at[tuple(place)].set(largest)


def block_scale(own_key, extent, cuts, low, top_value):
    def one(dim, blocks):
        draws = jax.random.uniform(jax.random.fold_in(jax.random.fold_in(own_key, 6), dim), (blocks,), jnp.float32, low / len(cuts), top_value / len(cuts))
        return jnp.repeat(jnp.exp(draws), extent[dim] // blocks).reshape((-1,) + (1,) * (len(extent) - dim - 1))

    level = one(*cuts[0])
    for cut in cuts[1:]:
        level = level * one(*cut)
    return level


def normal_values(key, dims, scale, limit, shards=(), kind=jnp.bfloat16):
    gain = block_scale(key, dims, shards, -0.22, 0.18) if shards else 1.0
    values = jax.random.normal(key, dims, jnp.float32) * scale * gain
    return jnp.minimum(jnp.maximum(values, -limit), limit).astype(kind)


def setup_inputs(seed: int = 0) -> dict:
    key_of = jax.random.split(jax.random.key(seed), 13)
    feature_pool = normal_values(key_of[0], (N_GOSSIP, POOL, H, W, C), 1.0, 6.0, ((0, 16), (2, 2)))
    sample_ids = plant(jax.random.randint(key_of[1], (N_GOSSIP,), 0, POOL), jax.random.fold_in(key_of[1], 1), 0, POOL - 1).astype(jnp.int32)
    token_mask = plant((jax.random.randint(key_of[2], (N_GOSSIP, H, W), 0, 5) < 3).astype(jnp.int32), jax.random.fold_in(key_of[2], 1), 0, 1)
    step_index = jax.random.randint(key_of[3], (1,), 0, 1200).astype(jnp.int32)
    dw_kernel = normal_values(key_of[4], (7, 7, C), 49 ** -0.5, 0.875, (), jnp.float32)
    dw_bias = normal_values(key_of[5], (C,), 0.5, 3.0, (), jnp.float32)
    ln_gain = jnp.clip(1.0 + 0.18 * jax.random.normal(key_of[6], (C,), jnp.float32), 0.1, 1.9)
    ln_bias = normal_values(key_of[7], (C,), 0.5, 3.0, (), jnp.float32)
    w_in = draw_w_in(jax.random.fold_in(key_of[12], 71), 0)
    grn_gamma = normal_values(key_of[9], (N_GOSSIP, HID), 0.5, 3.0, ((0, 16), (1, 2)), jnp.float32)
    grn_beta = normal_values(key_of[10], (N_GOSSIP, HID), 0.5, 3.0, ((0, 16), (1, 2)), jnp.float32)
    w_out = normal_values(key_of[11], (N_GOSSIP, HID, C), HID ** -0.5, 0.109375, ((0, 16), (1, 2)))
    return {"feature_pool": feature_pool, "sample_ids": sample_ids, "token_mask": token_mask, "step_index": step_index, "dw_kernel": dw_kernel, "dw_bias": dw_bias, "ln_gain": ln_gain, "ln_bias": ln_bias, "w_in": w_in, "grn_gamma": grn_gamma, "grn_beta": grn_beta, "w_out": w_out}


def depthwise(padded, kernel, bias_vec, height_rows, width_cols):
    result = jnp.zeros((height_rows, width_cols, kernel.shape[2]), jnp.float32)
    for i in range(7):
        for j in range(7):
            result = result + padded[i:i + height_rows, j:j + width_cols].astype(jnp.float32) * kernel[i, j]
    return result + bias_vec

def normalize(values, gain_vec, shift_vec):
    center = lax.optimization_barrier(jnp.mean(values, axis=-1, keepdims=True))
    spread = lax.optimization_barrier(jnp.mean(jnp.square(values - center), axis=-1, keepdims=True))
    return (values - center) * lax.rsqrt(spread + 1e-06) * gain_vec + shift_vec

def gelu_slope(pre_act):
    cdf_part = 0.5 * (1.0 + lax.erf(pre_act / math.sqrt(2.0)))
    pdf_part = jnp.exp(-0.5 * pre_act * pre_act) / math.sqrt(2.0 * math.pi)
    return cdf_part + pre_act * pdf_part

def group_grads(sample, keep, dw_kernel, dw_bias, ln_gain, ln_bias, w_in_group, gamma_vec, beta_vec, w_out_group):
    target = sample.astype(jnp.float32)
    masked = target * (1.0 - keep.astype(jnp.float32))[..., None]
    padded = jnp.pad(masked, ((3, 3), (3, 3), (0, 0)))
    normed = normalize(depthwise(padded, dw_kernel, dw_bias, H, W), ln_gain, ln_bias).astype(jnp.bfloat16).reshape(H * W, C)
    pre_act = jnp.dot(normed, w_in_group.T, preferred_element_type=jnp.float32)
    hidden = jax.nn.gelu(pre_act, approximate=False)
    norms = jnp.sqrt(lax.optimization_barrier(jnp.sum(hidden * hidden, axis=0)) + 1e-06)
    divisor = jnp.sum(norms) / HID + 1e-06
    ratio = norms / divisor
    mixed = (gamma_vec * (hidden * ratio) + beta_vec + hidden).astype(jnp.bfloat16)
    blocks = HID // N_SHARD
    parts = jnp.einsum('tkh,khc->ktc', mixed.astype(jnp.float32).reshape(H * W, N_SHARD, blocks), w_out_group.astype(jnp.float32).reshape(N_SHARD, blocks, C))
    rounded = lax.optimization_barrier(parts.astype(jnp.bfloat16))
    output = masked.reshape(H * W, C) + lax.optimization_barrier(jnp.sum(rounded.astype(jnp.float32), axis=0))
    errors = (keep.astype(jnp.float32).reshape(H * W, 1) * (output - target.reshape(H * W, C)) / math.sqrt(H * W)).astype(jnp.bfloat16)
    grad_out = jnp.dot(mixed.T, errors, preferred_element_type=jnp.float32)
    back = jnp.dot(errors, w_out_group.T, preferred_element_type=jnp.float32)
    grad_gamma = lax.optimization_barrier(jnp.sum(back * hidden * ratio, axis=0))
    grad_beta = lax.optimization_barrier(jnp.sum(back, axis=0))
    d_ratio = lax.optimization_barrier(jnp.sum(back * gamma_vec * hidden, axis=0))
    d_total = jnp.sum(d_ratio * (-norms / (divisor * divisor * HID)))
    d_norms = d_ratio / divisor + d_total
    d_hidden = back * (gamma_vec * ratio + 1.0) + d_norms / norms * hidden
    d_pre = (d_hidden * gelu_slope(pre_act)).astype(jnp.bfloat16)
    grad_in = jnp.dot(d_pre.T, normed, preferred_element_type=jnp.float32)
    return (grad_in, grad_out, grad_gamma, grad_beta)

def reference(feature_pool, sample_ids, token_mask, step_index, dw_kernel, dw_bias, ln_gain, ln_bias, w_in, grn_gamma, grn_beta, w_out):
    levels = N_GOSSIP.bit_length() - 1
    which_bit = (step_index[0] % levels).astype(jnp.int32)
    rotation = (step_index[0] // levels).astype(jnp.int32)
    span = jnp.left_shift(jnp.int32(1), which_bit)

    def one_group(group):
        pick = ((sample_ids[group] + rotation) % POOL).astype(jnp.int32)
        sample = feature_pool[group, pick]
        return group_grads(sample, token_mask[group], dw_kernel, dw_bias, ln_gain, ln_bias, w_in[group], grn_gamma[group], grn_beta[group], w_out[group])

    def pair_grads(index):
        lower = index // span * (2 * span) + index % span
        upper = lower + span
        first = one_group(lower)
        second = one_group(upper)
        return (((first[0] + second[0]) * 0.5).astype(jnp.bfloat16), ((first[1] + second[1]) * 0.5).astype(jnp.bfloat16), (first[2] + second[2]) * 0.5, (first[3] + second[3]) * 0.5)
    paired = lax.map(pair_grads, jnp.arange(N_GOSSIP // 2, dtype=jnp.int32))
    groups = jnp.arange(N_GOSSIP, dtype=jnp.int32)
    pair_of = (groups // (2 * span) * span + groups % span).astype(jnp.int32)
    return (paired[0][pair_of], paired[1][pair_of], paired[2][pair_of], paired[3][pair_of])
```

```python
from functools import partial
import math

import jax
import jax.numpy as jnp
from jax import lax
from jax.experimental import pallas as pl
from jax.experimental.pallas import tpu as pltpu
from jax.sharding import PartitionSpec as P

HID = 3072
H = 32
W = 32
POOL = 2
LANES = 128
F32 = jnp.float32
BF16 = jnp.bfloat16
NT = (((1,), (1,)), ((), ()))
TN = (((0,), (0,)), ((), ()))
NN = (((1,), (0,)), ((), ()))


def shape_of(dims, dtype):
    return jax.ShapeDtypeStruct(dims, dtype)


def whole(dims):
    return pl.BlockSpec(dims, lambda i: (0,) * len(dims))


def rows_at(block, width, offset=0):
    return pl.BlockSpec((block, width), lambda i: (i + offset, 0))


def call(kernel, grid, in_specs, out_specs, out_shape, scratch=(), aliases=None, flops=0, moved=0):
    return pl.pallas_call(
        kernel,
        grid=(grid,),
        in_specs=in_specs,
        out_specs=out_specs,
        out_shape=out_shape,
        scratch_shapes=list(scratch),
        input_output_aliases=aliases or {},
        compiler_params=pltpu.CompilerParams(
            dimension_semantics=("arbitrary",), vmem_limit_bytes=48 * 1024 * 1024
        ),
        cost_estimate=pl.CostEstimate(flops=flops, transcendentals=0, bytes_accessed=moved),
    )


def lane_tiles(width):
    return [slice(k * LANES, (k + 1) * LANES) for k in range(width // LANES)]


def folded(value):
    tiles = [value[:, t] for t in lane_tiles(value.shape[1])]
    return sum(tiles[1:], tiles[0])


def conv_kernel(me_ref, block_ref, edge_ref, live_ref, tap_ref, bias_ref, gain_ref, shift_ref,
                out_ref, pad_ref, conv_ref, *, own, blocks):
    c = pl.program_id(0)
    rows, cols, _ = block_ref.shape
    below = (me_ref[0] == 0) if own else (me_ref[0] == 1)
    inner = slice(8, 8 + cols)
    pad_ref[:, 0:8, :] = jnp.zeros((rows + 6, 8, LANES), F32)
    pad_ref[:, 8 + cols:, :] = jnp.zeros((rows + 6, 8, LANES), F32)
    pad_ref[3:3 + rows, inner, :] = block_ref[...].astype(F32) * live_ref[...]
    edge = edge_ref[...].astype(F32)
    pad_ref[0:3, inner, :] = jnp.where(below, 0.0, edge)
    pad_ref[3 + rows:, inner, :] = jnp.where(below, edge, 0.0)
    group = 8

    def one_group(g, carry):
        base = g * group
        acc = [jnp.broadcast_to(bias_ref[...], (cols, LANES)) for _ in range(group)]
        for j in range(7):
            for q in range(group + 6):
                x = pad_ref[base + q, 5 + j:5 + j + cols, :]
                for r in range(max(0, q - 6), min(group, q + 1)):
                    tap = (q - r) * 7 + j
                    acc[r] = acc[r] + x * tap_ref[tap:tap + 1, :]
        for r in range(group):
            conv_ref[c, pl.ds((base + r) * cols, cols), :] = acc[r]
        return carry

    lax.fori_loop(0, rows // group, one_group, 0)

    @pl.when(c == blocks - 1)
    def _():
        step = 32
        channels = blocks * LANES

        def one_step(t, carry):
            here = pl.ds(t * step, step)
            values = [conv_ref[k, here, :] for k in range(blocks)]
            center = jnp.sum(sum(values[1:], values[0]), axis=1, keepdims=True) / channels
            away = [v - center for v in values]
            squares = [d * d for d in away]
            spread = jnp.sum(sum(squares[1:], squares[0]), axis=1, keepdims=True) / channels
            inverse = lax.rsqrt(spread + 1e-06)
            for k, t_k in enumerate(lane_tiles(channels)):
                out_ref[here, t_k] = (
                    away[k] * inverse * gain_ref[:, t_k] + shift_ref[:, t_k]
                ).astype(BF16)
            return carry

        lax.fori_loop(0, rows * cols // step, one_step, 0)


def conv_norm(own, me, block, edge, live, taps, bias, gain, shift):
    rows, cols, channels = block.shape
    blocks = channels // LANES
    return call(
        partial(conv_kernel, own=own, blocks=blocks),
        blocks,
        [
            pl.BlockSpec(memory_space=pltpu.SMEM),
            pl.BlockSpec((rows, cols, LANES), lambda c: (0, 0, c)),
            pl.BlockSpec((3, cols, LANES), lambda c: (0, 0, c)),
            whole((rows, cols, LANES)),
            pl.BlockSpec((49, LANES), lambda c: (0, c)),
            pl.BlockSpec((1, LANES), lambda c: (0, c)),
            whole((1, channels)),
            whole((1, channels)),
        ],
        whole((rows * cols, channels)),
        shape_of((rows * cols, channels), BF16),
        [
            pltpu.VMEM((rows + 6, cols + 16, LANES), F32),
            pltpu.VMEM((blocks, rows * cols, LANES), F32),
        ],
        flops=98 * rows * cols * channels * 40,
        moved=4 * rows * cols * channels,
    )(me, block, edge, live, taps, bias, gain, shift)


def expand_block(normed_ref, w_ref, hidden_ref, slope_ref):
    pre_act = lax.dot_general(w_ref[...], normed_ref[...], NT, preferred_element_type=F32)
    cdf = 0.5 * (1.0 + lax.erf(pre_act * math.sqrt(0.5)))
    hidden = pre_act * cdf
    hidden_ref[...] = hidden
    slope_ref[...] = cdf + pre_act * (jnp.exp(-0.5 * pre_act * pre_act) * (1.0 / math.sqrt(2.0 * math.pi)))
    return folded(hidden * hidden)


def expand_first_kernel(normed_ref, w_ref, hidden_ref, slope_ref, square_ref):
    square_ref[...] = expand_block(normed_ref, w_ref, hidden_ref, slope_ref)


def expand_last_kernel(normed_ref, w_ref, before_ref, hidden_ref, slope_ref, norms_ref, total_ref):
    square = expand_block(normed_ref, w_ref, hidden_ref, slope_ref) + before_ref[...]
    norms = jnp.sqrt(jnp.sum(square, axis=1, keepdims=True) + 1e-06)
    norms_ref[...] = jnp.broadcast_to(norms, norms_ref.shape)

    @pl.when(pl.program_id(0) == 0)
    def _():
        total_ref[...] = jnp.zeros_like(total_ref)

    total_ref[...] += jnp.sum(norms)


def expand(normed, w, before=None):
    tokens, channels = normed.shape
    units = w.shape[0]
    block = 256
    last = before is not None
    wide, lane = rows_at(block, tokens), rows_at(block, LANES)
    out_specs = [wide, wide, lane] + [whole((8, LANES))] * last
    out_shape = [shape_of((units, tokens), F32)] * 2 + [shape_of((units, LANES), F32)]
    out_shape += [shape_of((8, LANES), F32)] * last
    return call(
        expand_last_kernel if last else expand_first_kernel,
        units // block,
        [whole((tokens, channels)), rows_at(block, channels)] + [lane] * last,
        out_specs,
        out_shape,
        flops=2 * tokens * channels * units * 2,
        moved=2 * units * channels + 8 * units * tokens,
    )(normed, w, *([before] if last else []))


def project_kernel(total_ref, peer_ref, norms_ref, gamma_ref, beta_ref, hidden_ref, w_ref,
                   mixed_ref, part_ref, acc_ref, *, steps, units_all):
    k = pl.program_id(0)
    divisor = (total_ref[0:1, :] + peer_ref[0:1, :]) / units_all + 1e-06
    scale = gamma_ref[...] * (norms_ref[...] / divisor) + 1.0
    shift = beta_ref[...]
    for t in lane_tiles(hidden_ref.shape[1]):
        mixed_ref[:, t] = (hidden_ref[:, t] * scale + shift).astype(BF16)
    product = lax.dot_general(mixed_ref[...], w_ref[...], TN, preferred_element_type=F32)

    @pl.when(k == 0)
    def _():
        acc_ref[...] = product

    @pl.when(k > 0)
    def _():
        acc_ref[...] += product

    @pl.when(k == steps - 1)
    def _():
        part_ref[...] = acc_ref[...].astype(BF16)


def project(total, peer, norms, gamma, beta, hidden, w, units_all):
    units, tokens = hidden.shape
    channels = w.shape[1]
    block = 512
    lane, tiny = rows_at(block, LANES), whole((8, LANES))
    return call(
        partial(project_kernel, steps=units // block, units_all=units_all),
        units // block,
        [tiny, tiny, lane, lane, lane, rows_at(block, tokens), rows_at(block, channels)],
        [rows_at(block, tokens), whole((tokens, channels))],
        [shape_of((units, tokens), BF16), shape_of((tokens, channels), BF16)],
        [pltpu.VMEM((tokens, channels), F32)],
        flops=2 * tokens * channels * units * 2,
        moved=2 * units * channels + 6 * units * tokens,
    )(total, peer, norms, gamma, beta, hidden, w)


def back_block(part_ref, peer_ref, target_ref, live_ref, w_ref, hidden_ref, errors_ref, back_ref, scale):
    @pl.when(pl.program_id(0) == 0)
    def _():
        live = live_ref[...]
        keep = (1.0 - live) * scale
        for t in lane_tiles(target_ref.shape[1]):
            target = target_ref[:, t].astype(F32)
            summed = part_ref[:, t].astype(F32) + peer_ref[:, t].astype(F32)
            errors_ref[:, t] = (keep * (target * live + summed - target)).astype(BF16)

    back = lax.dot_general(w_ref[...], errors_ref[...], NT, preferred_element_type=F32)
    back_ref[...] = back
    return folded(back), folded(back * hidden_ref[...])


def back_first_kernel(part_ref, peer_ref, target_ref, live_ref, w_ref, hidden_ref,
                      errors_ref, back_ref, sum_ref, dot_ref, *, scale):
    sum_ref[...], dot_ref[...] = back_block(
        part_ref, peer_ref, target_ref, live_ref, w_ref, hidden_ref, errors_ref, back_ref, scale
    )


def back_last_kernel(part_ref, peer_ref, target_ref, live_ref, w_ref, hidden_ref,
                     sum_before_ref, dot_before_ref, total_ref, peer_total_ref, norms_ref, gamma_ref,
                     errors_ref, back_ref, beta_out_ref, gamma_out_ref, dots_ref, slope_ref, *, scale, units_all):
    sums, dots = back_block(
        part_ref, peer_ref, target_ref, live_ref, w_ref, hidden_ref, errors_ref, back_ref, scale
    )
    lanes = beta_out_ref.shape
    sums = jnp.sum(sums + sum_before_ref[...], axis=1, keepdims=True)
    dots = jnp.broadcast_to(jnp.sum(dots + dot_before_ref[...], axis=1, keepdims=True), lanes)
    divisor = (total_ref[0:1, :] + peer_total_ref[0:1, :]) / units_all + 1e-06
    norms = norms_ref[...]
    beta_out_ref[...] = jnp.broadcast_to(sums, lanes)
    gamma_out_ref[...] = dots * (norms / divisor)
    dots_ref[...] = dots
    slopes = dots * gamma_ref[...] * (-norms / (divisor * divisor * units_all))

    @pl.when(pl.program_id(0) == 0)
    def _():
        slope_ref[...] = jnp.zeros_like(slope_ref)

    slope_ref[...] += jnp.sum(slopes[:, 0:1])


def back_pass(part, peer, target, live, w, hidden, scale, units_all, more=None):
    tokens, channels = part.shape
    units = w.shape[0]
    block = 256
    lane, tiny, full = rows_at(block, LANES), whole((8, LANES)), whole((tokens, channels))
    in_specs = [full, full, full, whole((tokens, LANES)), rows_at(block, channels), rows_at(block, tokens)]
    out_specs = [full, rows_at(block, tokens), lane, lane]
    out_shape = [shape_of((tokens, channels), BF16), shape_of((units, tokens), F32)]
    out_shape += [shape_of((units, LANES), F32)] * 2
    kernel = partial(back_first_kernel, scale=scale)
    if more is not None:
        kernel = partial(back_last_kernel, scale=scale, units_all=units_all)
        in_specs += [lane, lane, tiny, tiny, lane, lane]
        out_specs += [lane, tiny]
        out_shape += [shape_of((units, LANES), F32), shape_of((8, LANES), F32)]
    return call(
        kernel, units // block, in_specs, out_specs, out_shape,
        flops=2 * tokens * channels * units * 2,
        moved=2 * units * channels + 8 * units * tokens,
    )(part, peer, target, live, w, hidden, *(more or ()))


def pre_grad_kernel(total_ref, peer_ref, slope_ref, peer_slope_ref, norms_ref, gamma_ref, dots_ref,
                    back_a, back_b, hidden_a, hidden_b, bend_a, bend_b, out_ref, *, units_all):
    divisor = (total_ref[0:1, :] + peer_ref[0:1, :]) / units_all + 1e-06
    d_total = slope_ref[0:1, :] + peer_slope_ref[0:1, :]
    norms = norms_ref[...]
    gamma = gamma_ref[...]
    ratio = norms / divisor
    along = gamma * ratio + 1.0
    across = (gamma * dots_ref[...] / divisor + d_total) / norms
    tokens = back_a.shape[1]
    for base, back, hidden, bend in ((0, back_a, hidden_a, bend_a), (tokens, back_b, hidden_b, bend_b)):
        for t in lane_tiles(tokens):
            value = (back[:, t] * along + across * hidden[:, t]) * bend[:, t]
            out_ref[:, base + t.start:base + t.stop] = value.astype(BF16)


def pre_grad(first, count, total, peer, slope, peer_slope, norms, gamma, dots, backs, hiddens, bends, units_all):
    tokens = backs[0].shape[1]
    block = 128
    at = first // block
    lane, tiny, wide = rows_at(block, LANES, at), whole((8, LANES)), rows_at(block, tokens, at)
    return call(
        partial(pre_grad_kernel, units_all=units_all),
        count // block,
        [tiny] * 4 + [lane] * 3 + [wide] * 6,
        rows_at(block, 2 * tokens),
        shape_of((count, 2 * tokens), BF16),
        flops=count * tokens * 2 * 100,
        moved=count * tokens * 28,
    )(total, peer, slope, peer_slope, norms, gamma, dots, *backs, *hiddens, *bends)


def pair_out_kernel(mix_a, mix_b, mix_c, mix_d, err_a, err_b, err_c, err_d, out_ref):
    total = lax.dot_general(mix_a[...], err_a[...], NN, preferred_element_type=F32)
    for mix, err in ((mix_b, err_b), (mix_c, err_c), (mix_d, err_d)):
        total += lax.dot_general(mix[...], err[...], NN, preferred_element_type=F32)
    out_ref[...] = (total * 0.5).astype(BF16)


def pair_out(mixed, errors):
    units, tokens = mixed[0].shape
    channels = errors[0].shape[1]
    block = 256
    return call(
        pair_out_kernel,
        units // block,
        [rows_at(block, tokens)] * 4 + [whole((tokens, channels))] * 4,
        rows_at(block, channels),
        shape_of((units, channels), BF16),
        flops=8 * tokens * channels * units * 2,
        moved=8 * units * tokens + 2 * units * channels + 8 * tokens * channels,
    )(*mixed, *errors)


def pair_in_kernel(own_ref, peer_ref, norm_a, norm_b, norm_c, norm_d, *refs):
    out_ref = refs[-1]
    tokens = norm_a.shape[0]
    total = lax.dot_general(own_ref[:, :tokens], norm_a[...], NN, preferred_element_type=F32)
    total += lax.dot_general(own_ref[:, tokens:], norm_b[...], NN, preferred_element_type=F32)
    total += lax.dot_general(peer_ref[:, :tokens], norm_c[...], NN, preferred_element_type=F32)
    total += lax.dot_general(peer_ref[:, tokens:], norm_d[...], NN, preferred_element_type=F32)
    out_ref[...] = (total * 0.5).astype(BF16)


def pair_in(first, units, own, peer, normed, filled):
    count, tokens = own.shape
    channels = normed[0].shape[1]
    block = 128
    held = [] if filled is None else [filled]
    return call(
        pair_in_kernel,
        count // block,
        [rows_at(block, tokens)] * 2 + [whole((tokens // 2, channels))] * 4
        + [pl.BlockSpec(memory_space=pl.ANY)] * len(held),
        rows_at(block, channels, first // block),
        shape_of((units, channels), BF16),
        aliases={6: 0} if held else None,
        flops=4 * tokens * channels * count * 2,
        moved=4 * count * tokens + 2 * count * channels + 4 * tokens * channels,
    )(own, peer, *normed, *held)


def after(value, *needed):
    place = pl.BlockSpec(memory_space=pl.ANY)
    return pl.pallas_call(
        lambda *refs: None,
        in_specs=[place] * (1 + len(needed)),
        out_specs=place,
        out_shape=shape_of(value.shape, value.dtype),
        input_output_aliases={0: 0},
    )(value, *needed)


def pair_body(bit, sample, token_mask, me, dw_kernel, dw_bias, ln_gain, ln_bias, w_in, grn_gamma, grn_beta, w_out):
    rows, cols, channels = sample.shape
    units = w_in.shape[0]
    units_all = 2 * units
    tokens = rows * cols
    scale = 1.0 / math.sqrt(2 * tokens)
    direct = bit == 0

    def across(value):
        return lax.ppermute(value, "shard", [(0, 1), (1, 0)])

    def to_peer(value):
        return lax.ppermute(value, "gossip", [(i, i ^ 1 << bit) for i in range(lax.axis_size("gossip"))])

    def live_of(keep):
        return jnp.broadcast_to((1.0 - keep.astype(F32))[..., None], (rows, cols, LANES))

    first = jnp.where(me == 0, rows - 3, 0)
    live = live_of(token_mask)
    edge = lax.dynamic_slice_in_dim(sample, first, 3, axis=0).astype(F32)
    edge = (edge * (1.0 - lax.dynamic_slice_in_dim(token_mask, first, 3, axis=0).astype(F32))[..., None]).astype(BF16)
    edge_other = across(edge)
    mask_other = across(token_mask)
    sample_other = across(sample)
    live_other = live_of(mask_other)
    taps = dw_kernel.reshape(49, channels)
    vectors = [v.reshape(1, channels) for v in (dw_bias, ln_gain, ln_bias)]
    gamma = jnp.broadcast_to(grn_gamma[:, None], (units, LANES))
    beta = jnp.broadcast_to(grn_beta[:, None], (units, LANES))
    me_vec = me.reshape(1)

    normed_own = conv_norm(True, me_vec, sample, edge_other, live, taps, *vectors)
    normed_own_p = to_peer(normed_own)
    hidden_own, bend_own, squares = expand(normed_own, w_in)
    normed_other = conv_norm(False, me_vec, sample_other, edge, live_other, taps, *vectors)
    hidden_other, bend_other, norms, total = expand(normed_other, w_in, squares)
    total_x = across(total)

    mixed_other, part_other = project(total, total_x, norms, gamma, beta, hidden_other, w_out, units_all)
    came_own = across(part_other)
    mixed_other_p = to_peer(mixed_other)
    mixed_own, part_own = project(total, total_x, norms, gamma, beta, hidden_own, w_out, units_all)
    came_other = across(part_own)
    mixed_own_p = to_peer(mixed_own)

    errors_own, back_own, sums, dots = back_pass(
        part_own, came_own, sample.reshape(tokens, channels), live.reshape(tokens, LANES),
        w_out, hidden_own, scale, units_all,
    )
    errors_own_p = to_peer(errors_own)
    errors_other, back_other, g_beta, g_gamma, dots, slope = back_pass(
        part_other, came_other, sample_other.reshape(tokens, channels), live_other.reshape(tokens, LANES),
        w_out, hidden_other, scale, units_all, (sums, dots, total, total_x, norms, gamma),
    )
    slope_x = across(slope)
    if direct:
        normed_other_p = to_peer(normed_other)
        errors_other_p = to_peer(errors_other)
    else:
        normed_other_p = across(after(normed_own_p, came_other))
        errors_other_p = across(errors_own_p)
    small = jnp.stack([g_gamma[:, 0], g_beta[:, 0]])
    small = (small + to_peer(small)) * 0.5

    count = units // 4
    pieces = []
    for n in range(4):
        own = pre_grad(
            n * count, count, total, total_x, slope, slope_x, norms, gamma, dots,
            (back_own, back_other), (hidden_own, hidden_other), (bend_own, bend_other), units_all,
        )
        pieces.append((own, to_peer(own)))
    grad_out = pair_out(
        (mixed_own, mixed_other, mixed_own_p, mixed_other_p),
        (errors_own, errors_other, errors_own_p, errors_other_p),
    )
    grad_in = None
    normed = (normed_own, normed_other, normed_own_p, normed_other_p)
    for n, (own, peer) in enumerate(pieces):
        grad_in = pair_in(n * count, units, own, peer, normed, grad_in)
    return grad_in, grad_out, small[0], small[1]


def shortened(value):

    def short(part):
        return part.astype(jnp.bfloat16) if part.dtype == jnp.float32 else part

    return jax.tree.map(short, value)


def from_partner(value, axis, distance):
    return lax.ppermute(value, axis, [(i, i ^ 1 << distance) for i in range(lax.axis_size(axis))])


def with_halo(block, sides, width):
    for axis, dim in sides:
        count = lax.axis_size(axis)
        forward = [(i, i + 1) for i in range(count - 1)]
        backward = [(target, source) for source, target in forward]
        low = lax.ppermute(
            lax.slice_in_dim(block, block.shape[dim] - width, None, axis=dim), axis, forward
        )
        high = lax.ppermute(lax.slice_in_dim(block, 0, width, axis=dim), axis, backward)
        block = jnp.concatenate([low, block, high], axis=dim)
    return block


def depthwise(padded, kernel, bias_vec, height_rows, width_cols):
    result = jnp.zeros((height_rows, width_cols, kernel.shape[2]), jnp.float32)
    for i in range(7):
        for j in range(7):
            result = (
                result
                + padded[i : i + height_rows, j : j + width_cols].astype(jnp.float32) * kernel[i, j]
            )
    return result + bias_vec


def normalize(values, gain_vec, shift_vec):
    center = jnp.mean(values, axis=-1, keepdims=True)
    spread = jnp.mean(jnp.square(values - center), axis=-1, keepdims=True)
    return (values - center) * lax.rsqrt(spread + 1e-06) * gain_vec + shift_vec


def gelu_slope(pre_act):
    cdf_part = 0.5 * (1.0 + lax.erf(pre_act / math.sqrt(2.0)))
    pdf_part = jnp.exp(-0.5 * pre_act * pre_act) / math.sqrt(2.0 * math.pi)
    return cdf_part + pre_act * pdf_part


def peer_swap(payload, which_bit):
    return jax.tree.map(
        lambda part, own: part.astype(own.dtype),
        from_partner(shortened(payload), "gossip", which_bit),
        payload,
    )


def general_body(
    feature_pool,
    sample_ids,
    token_mask,
    step_index,
    dw_kernel,
    dw_bias,
    ln_gain,
    ln_bias,
    w_in,
    grn_gamma,
    grn_beta,
    w_out,
):
    levels = lax.axis_size("gossip").bit_length() - 1
    rotation = step_index[0] // levels
    pick = (sample_ids[0] + rotation) % POOL
    sample = lax.dynamic_index_in_dim(feature_pool[0], pick, 0, keepdims=False)
    keep = token_mask[0]
    local_rows, width_cols, channels = sample.shape
    w_in_local = w_in[0]
    w_out_local = w_out[0]
    gamma_vec = grn_gamma[0]
    beta_vec = grn_beta[0]
    error_scale = 1.0 / math.sqrt(H * W)
    masked = (sample.astype(jnp.float32) * (1.0 - keep.astype(jnp.float32))[..., None]).astype(
        jnp.bfloat16
    )
    rimmed = with_halo(masked, (("shard", 0),), 3)
    padded = jnp.pad(rimmed, ((0, 0), (3, 3), (0, 0)))
    normed = (
        normalize(depthwise(padded, dw_kernel, dw_bias, local_rows, width_cols), ln_gain, ln_bias)
        .astype(jnp.bfloat16)
        .reshape(-1, channels)
    )
    gathered = lax.all_gather(normed, "shard", axis=0, tiled=True)
    pre_act = lax.dot_general(
        gathered, w_in_local, (((1,), (1,)), ((), ())), preferred_element_type=jnp.float32
    )
    hidden = jax.nn.gelu(pre_act, approximate=False)
    norms = jnp.sqrt(jnp.sum(hidden * hidden, axis=0) + 1e-06)
    norm_total = lax.psum(jnp.sum(norms), "shard")
    divisor = norm_total / HID + 1e-06
    ratio = norms / divisor
    mixed = (gamma_vec * (hidden * ratio) + beta_vec + hidden).astype(jnp.bfloat16)
    own_sum = lax.psum_scatter(
        jnp.dot(mixed, w_out_local, preferred_element_type=jnp.float32).astype(jnp.bfloat16),
        "shard",
        scatter_dimension=0,
        tiled=True,
    ).astype(jnp.float32)
    output_own = masked.astype(jnp.float32).reshape(-1, channels) + own_sum
    target_own = sample.astype(jnp.float32).reshape(-1, channels)
    errors_own = (
        keep.astype(jnp.float32).reshape(-1, 1) * (output_own - target_own) * error_scale
    ).astype(jnp.bfloat16)
    errors_all = lax.all_gather(errors_own, "shard", axis=0, tiled=True)
    grad_out_local = lax.dot_general(
        mixed, errors_all, (((0,), (0,)), ((), ())), preferred_element_type=jnp.float32
    )
    back = lax.dot_general(
        errors_all, w_out_local, (((1,), (1,)), ((), ())), preferred_element_type=jnp.float32
    )
    grad_gamma_local = jnp.sum(back * hidden * ratio, axis=0)
    grad_beta_local = jnp.sum(back, axis=0)
    d_ratio = jnp.sum(back * gamma_vec * hidden, axis=0)
    slope_local = jnp.sum(d_ratio * (-norms / (divisor * divisor * HID)))
    d_total = lax.psum(slope_local, "shard")
    d_norms = d_ratio / divisor + d_total
    d_hidden = back * (gamma_vec * ratio + 1.0) + d_norms / norms * hidden
    d_pre = (d_hidden * gelu_slope(pre_act)).astype(jnp.bfloat16)
    grad_in_local = lax.dot_general(
        d_pre, gathered, (((0,), (0,)), ((), ())), preferred_element_type=jnp.float32
    )
    own_grads = (grad_in_local, grad_out_local, grad_gamma_local, grad_beta_local)
    branches = [partial(peer_swap, which_bit=b) for b in range(levels)]
    peer_grads = lax.switch(step_index[0] % levels, branches, own_grads)
    grad_in = ((own_grads[0] + peer_grads[0]) * 0.5).astype(jnp.bfloat16)
    grad_out = ((own_grads[1] + peer_grads[1]) * 0.5).astype(jnp.bfloat16)
    grad_gamma = (own_grads[2] + peer_grads[2]) * 0.5
    grad_beta = (own_grads[3] + peer_grads[3]) * 0.5
    return (grad_in[None], grad_out[None], grad_gamma[None], grad_beta[None])


def body(
    feature_pool,
    sample_ids,
    token_mask,
    step_index,
    dw_kernel,
    dw_bias,
    ln_gain,
    ln_bias,
    w_in,
    grn_gamma,
    grn_beta,
    w_out,
):
    if lax.axis_size("shard") != 2:
        return general_body(
            feature_pool, sample_ids, token_mask, step_index, dw_kernel, dw_bias,
            ln_gain, ln_bias, w_in, grn_gamma, grn_beta, w_out,
        )
    levels = lax.axis_size("gossip").bit_length() - 1
    pick = (sample_ids[0] + step_index[0] // levels) % feature_pool.shape[1]
    sample = lax.dynamic_index_in_dim(feature_pool[0], pick, 0, keepdims=False)
    me = lax.axis_index("shard").astype(jnp.int32)
    outs = lax.switch(
        step_index[0] % levels,
        [partial(pair_body, bit) for bit in range(levels)],
        sample, token_mask[0], me, dw_kernel, dw_bias, ln_gain, ln_bias,
        w_in[0], grn_gamma[0], grn_beta[0], w_out[0],
    )
    return tuple(out[None] for out in outs)


def solution(mesh):
    in_specs = (
        P("gossip", None, "shard", None, None),
        P("gossip"),
        P("gossip", "shard", None),
        P(),
        P(),
        P(),
        P(),
        P(),
        P("gossip", "shard", None),
        P("gossip", "shard"),
        P("gossip", "shard"),
        P("gossip", "shard", None),
    )
    out_specs = (
        P("gossip", "shard", None),
        P("gossip", "shard", None),
        P("gossip", "shard"),
        P("gossip", "shard"),
    )
    return jax.shard_map(body, mesh=mesh, in_specs=in_specs, out_specs=out_specs, check_vma=False)
```

```python
from functools import partial
import math

import jax
import jax.numpy as jnp
from jax import lax
from jax.experimental import pallas as pl
from jax.experimental.pallas import tpu as pltpu
from jax.sharding import PartitionSpec as P

HID = 3072
H = 32
W = 32
POOL = 2
LANES = 128
F32 = jnp.float32
BF16 = jnp.bfloat16
NT = (((1,), (1,)), ((), ()))
TN = (((0,), (0,)), ((), ()))
NN = (((1,), (0,)), ((), ()))


def shape_of(dims, dtype):
    return jax.ShapeDtypeStruct(dims, dtype)


def whole(dims):
    return pl.BlockSpec(dims, lambda i: (0,) * len(dims))


def rows_at(block, width, offset=0):
    return pl.BlockSpec((block, width), lambda i: (i + offset, 0))


def call(kernel, grid, in_specs, out_specs, out_shape, scratch=(), aliases=None, needed=()):
    inputs, extra = len(in_specs), len(needed)

    def run(*refs):
        kernel(*refs[:inputs], *refs[inputs + extra:])

    def placed(shape):
        return pltpu.HBM(shape.shape, shape.dtype) if math.prod(shape.shape) > 1 << 16 else shape

    single = not isinstance(out_shape, list)
    held = placed(out_shape) if single else [placed(s) for s in out_shape]
    built = pl.pallas_call(
        run,
        grid=(grid,),
        in_specs=list(in_specs) + [pl.BlockSpec(memory_space=pl.ANY)] * extra,
        out_specs=out_specs,
        out_shape=held,
        scratch_shapes=list(scratch),
        input_output_aliases=aliases or {},
        compiler_params=pltpu.CompilerParams(
            dimension_semantics=("arbitrary",), vmem_limit_bytes=48 * 1024 * 1024
        ),
    )
    def in_hbm(value):
        return pltpu.with_memory_space_constraint(value, pltpu.HBM) if value.size > 1 << 16 else value

    return lambda *args: built(*map(in_hbm, args), *map(in_hbm, needed))


def lane_tiles(width):
    return [slice(k * LANES, (k + 1) * LANES) for k in range(width // LANES)]


def folded(value):
    tiles = [value[:, t] for t in lane_tiles(value.shape[1])]
    return sum(tiles[1:], tiles[0])


def conv_kernel(me_ref, live_own_ref, live_other_ref, tap_ref, bias_ref, gain_ref, shift_ref, *refs,
                parts, out_rows, half, copies, held):
    scratch = 4 + bool(copies)
    outs = 1 + bool(copies)
    sources = refs[:len(refs) - scratch - outs - held]
    out_ref = refs[-scratch - outs]
    pad_ref, conv_ref, norm_ref, sems = refs[-scratch:len(refs) - scratch + 4]
    rows, cols, _ = live_own_ref.shape
    blocks = conv_ref.shape[0]
    window = out_rows + 6
    upper = me_ref[0] == 0
    inner = slice(8, 8 + cols)
    moves = []
    if copies:
        map_ref, map_sems = refs[-scratch - 1], refs[-1]
        for n, (source, at, mirrored) in enumerate(copies):
            there = pl.ds(jnp.where(upper, at, mirrored), sources[source].shape[0])
            moves.append(pltpu.make_async_copy(sources[source], map_ref.at[there], map_sems.at[n]))
            moves[-1].start()
    pad_ref[:, 0:8, :] = jnp.zeros((window, 8, LANES), F32)
    pad_ref[:, 8 + cols:, :] = jnp.zeros((window, 8, LANES), F32)
    group = 8

    def one_block(c, carry):
        lane = pl.ds(pl.multiple_of(c * LANES, LANES), LANES)
        for source, count, distance, place in parts:
            there = pl.ds(jnp.where(upper, place, window - count - place), count)
            if source is None:
                pad_ref[there, inner, :] = jnp.zeros((count, cols, LANES), F32)
                continue
            own = distance < 0
            live_ref = live_own_ref if own else live_other_ref
            first = jnp.where(upper, distance + rows if own else distance,
                              -distance - count if own else rows - distance - count)
            length = sources[source].shape[0]
            values = sources[source][pl.ds(jnp.where(upper, length - count, 0), count), :, lane]
            pad_ref[there, inner, :] = values.astype(F32) * live_ref[pl.ds(first, count)]

        def one_group(g, carry):
            base = g * group
            acc = [jnp.broadcast_to(bias_ref[:, lane], (cols, LANES)) for _ in range(group)]
            for j in range(7):
                for q in range(group + 6):
                    x = pad_ref[base + q, 5 + j:5 + j + cols, :]
                    for r in range(max(0, q - 6), min(group, q + 1)):
                        tap = (q - r) * 7 + j
                        acc[r] = acc[r] + x * tap_ref[tap:tap + 1, lane]
            for r in range(group):
                conv_ref[c, pl.ds((base + r) * cols, cols), :] = acc[r]
            return carry

        return lax.fori_loop(0, out_rows // group, one_group, carry)

    lax.fori_loop(0, blocks, one_block, 0)
    step = 32
    channels = blocks * LANES
    base = 0
    if half is not None:
        base = jnp.where(upper, half, 1 - half) * (out_rows * cols)

    def one_step(t, carry):
        here = pl.ds(pl.multiple_of(t * step, step), step)
        values = [conv_ref[k, here, :] for k in range(blocks)]
        center = jnp.sum(sum(values[1:], values[0]), axis=1, keepdims=True) / channels
        away = [v - center for v in values]
        squares = [d * d for d in away]
        spread = jnp.sum(sum(squares[1:], squares[0]), axis=1, keepdims=True) / channels
        inverse = lax.rsqrt(spread + 1e-06)
        for k, t_k in enumerate(lane_tiles(channels)):
            norm_ref[here, t_k] = (away[k] * inverse * gain_ref[:, t_k] + shift_ref[:, t_k]).astype(BF16)
        return carry

    quarter = out_rows * cols // 4
    for n in range(4):
        lax.fori_loop(n * quarter // step, (n + 1) * quarter // step, one_step, 0)
        there = pl.ds(pl.multiple_of(base + n * quarter, quarter), quarter)
        moves.append(pltpu.make_async_copy(norm_ref.at[n * quarter:(n + 1) * quarter], out_ref.at[there], sems.at[n]))
        moves[-1].start()
    for move in moves:
        move.wait()


def conv_norm(me, lives, maps, parts, half, vectors, copies=(), filled=(), needed=()):
    rows, cols = lives[0].shape[:2]
    channels = vectors[0].shape[1]
    blocks = channels // LANES
    out_rows = rows if half is None else rows // 2
    inputs = 7 + len(maps)
    held = len(filled)
    place = pl.BlockSpec(memory_space=pltpu.HBM)
    more = bool(copies)
    return call(
        partial(conv_kernel, parts=parts, out_rows=out_rows, half=half, copies=copies, held=held),
        1,
        [pl.BlockSpec(memory_space=pltpu.SMEM)]
        + [whole(v.shape) for v in (*lives, *vectors, *maps)]
        + [pl.BlockSpec(memory_space=pl.ANY)] * held,
        [place] * (1 + more),
        [shape_of((rows * cols, channels), BF16)] + [shape_of((rows, cols, channels), BF16)] * more,
        [
            pltpu.VMEM((out_rows + 6, cols + 16, LANES), F32),
            pltpu.VMEM((blocks, out_rows * cols, LANES), F32),
            pltpu.VMEM((out_rows * cols, channels), BF16),
            pltpu.SemaphoreType.DMA((4,)),
        ] + [pltpu.SemaphoreType.DMA((len(copies),))] * more,
        aliases={inputs: 0} if held else None,
        needed=needed,
    )(me, *lives, *vectors, *maps, *filled)


def columns_kernel(gamma_ref, beta_ref, gamma_out, beta_out):
    for row, out in ((gamma_ref, gamma_out), (beta_ref, beta_out)):
        out[...] = jnp.broadcast_to(row[...], (LANES, row.shape[1])).T


def columns(gamma, beta):
    units = gamma.shape[0]
    return call(
        columns_kernel, 1, [whole((1, units))] * 2, [whole((units, LANES))] * 2,
        [shape_of((units, LANES), F32)] * 2,
    )(gamma[None], beta[None])


def expand_block(normed_ref, w_ref, hidden_ref, slope_ref):
    pre_act = lax.dot_general(w_ref[...], normed_ref[...], NT, preferred_element_type=F32)
    cdf = 0.5 * (1.0 + lax.erf(pre_act * math.sqrt(0.5)))
    hidden = pre_act * cdf
    hidden_ref[...] = hidden.astype(BF16)
    slope = cdf + pre_act * (jnp.exp(-0.5 * pre_act * pre_act) * (1.0 / math.sqrt(2.0 * math.pi)))
    slope_ref[...] = slope.astype(BF16)
    return folded(hidden * hidden)


def expand_first_kernel(normed_ref, w_ref, hidden_ref, slope_ref, square_ref):
    square_ref[...] = expand_block(normed_ref, w_ref, hidden_ref, slope_ref)


def expand_last_kernel(normed_ref, w_ref, before_ref, hidden_ref, slope_ref, norms_ref, total_ref):
    square = expand_block(normed_ref, w_ref, hidden_ref, slope_ref) + before_ref[...]
    norms = jnp.sqrt(jnp.sum(square, axis=1, keepdims=True) + 1e-06)
    norms_ref[...] = jnp.broadcast_to(norms, norms_ref.shape)

    @pl.when(pl.program_id(0) == 0)
    def _():
        total_ref[...] = jnp.zeros_like(total_ref)

    total_ref[...] += jnp.sum(norms)


def expand(normed, w, before=None, needed=()):
    tokens, channels = normed.shape
    units = w.shape[0]
    block = 512
    last = before is not None
    wide, lane = rows_at(block, tokens), rows_at(block, LANES)
    out_specs = [wide, wide, lane] + [whole((8, LANES))] * last
    out_shape = [shape_of((units, tokens), BF16)] * 2 + [shape_of((units, LANES), F32)]
    out_shape += [shape_of((8, LANES), F32)] * last
    return call(
        expand_last_kernel if last else expand_first_kernel,
        units // block,
        [whole((tokens, channels)), rows_at(block, channels)] + [lane] * last,
        out_specs,
        out_shape,
        needed=needed,
    )(normed, w, *([before] if last else []))


def project_kernel(total_ref, peer_ref, norms_ref, gamma_ref, beta_ref, hidden_own_ref, hidden_other_ref, w_ref,
                   mixed_ref, part_own_ref, part_other_ref, acc_ref, *, steps, units_all):
    k = pl.program_id(0)
    divisor = (total_ref[0:1, :] + peer_ref[0:1, :]) / units_all + 1e-06
    scale = gamma_ref[...] * (norms_ref[...] / divisor) + 1.0
    shift = beta_ref[...]
    tokens = hidden_own_ref.shape[1]
    for base, hidden_ref in ((0, hidden_own_ref), (tokens, hidden_other_ref)):
        for t in lane_tiles(tokens):
            value = hidden_ref[:, t].astype(F32) * scale + shift
            mixed_ref[:, base + t.start:base + t.stop] = value.astype(BF16)
    for n, part_ref in ((0, part_own_ref), (1, part_other_ref)):
        product = lax.dot_general(
            mixed_ref[:, n * tokens:(n + 1) * tokens], w_ref[...], TN, preferred_element_type=F32
        )

        @pl.when(k == 0)
        def _():
            acc_ref[n] = product

        @pl.when((k > 0) & (k < steps - 1))
        def _():
            acc_ref[n] += product

        @pl.when(k == steps - 1)
        def _():
            part_ref[...] = (acc_ref[n] + product).astype(BF16)


def project(total, peer, norms, gamma, beta, hiddens, w, units_all, needed=()):
    units, tokens = hiddens[0].shape
    channels = w.shape[1]
    block = 512
    lane, tiny, part = rows_at(block, LANES), whole((8, LANES)), whole((tokens, channels))
    return call(
        partial(project_kernel, steps=units // block, units_all=units_all),
        units // block,
        [tiny, tiny, lane, lane, lane, rows_at(block, tokens), rows_at(block, tokens), rows_at(block, channels)],
        [rows_at(block, 2 * tokens), part, part],
        [shape_of((units, 2 * tokens), BF16)] + [shape_of((tokens, channels), BF16)] * 2,
        [pltpu.VMEM((2, tokens, channels), F32)],
        needed=needed,
    )(total, peer, norms, gamma, beta, *hiddens, w)


def back_block(part_ref, peer_ref, target_ref, live_ref, w_ref, hidden_ref, errors_ref, back_ref, scale):
    @pl.when(pl.program_id(0) == 0)
    def _():
        live = live_ref[...]
        keep = (1.0 - live) * scale
        for t in lane_tiles(target_ref.shape[1]):
            target = target_ref[:, t].astype(F32)
            summed = part_ref[:, t].astype(F32) + peer_ref[:, t].astype(F32)
            errors_ref[:, t] = (keep * (target * live + summed - target)).astype(BF16)

    back = lax.dot_general(w_ref[...], errors_ref[...], NT, preferred_element_type=F32)
    back_ref[...] = back.astype(BF16)
    return folded(back), folded(back * hidden_ref[...].astype(F32))


def back_first_kernel(part_ref, peer_ref, target_ref, live_ref, w_ref, hidden_ref,
                      errors_ref, back_ref, sum_ref, dot_ref, *, scale):
    sum_ref[...], dot_ref[...] = back_block(
        part_ref, peer_ref, target_ref, live_ref, w_ref, hidden_ref, errors_ref, back_ref, scale
    )


def back_last_kernel(part_ref, peer_ref, target_ref, live_ref, w_ref, hidden_ref,
                     sum_before_ref, dot_before_ref, total_ref, peer_total_ref, norms_ref, gamma_ref,
                     errors_ref, back_ref, beta_out_ref, gamma_out_ref, dots_ref, slope_ref, *, scale, units_all):
    sums, dots = back_block(
        part_ref, peer_ref, target_ref, live_ref, w_ref, hidden_ref, errors_ref, back_ref, scale
    )
    lanes = beta_out_ref.shape
    sums = jnp.sum(sums + sum_before_ref[...], axis=1, keepdims=True)
    dots = jnp.broadcast_to(jnp.sum(dots + dot_before_ref[...], axis=1, keepdims=True), lanes)
    divisor = (total_ref[0:1, :] + peer_total_ref[0:1, :]) / units_all + 1e-06
    norms = norms_ref[...]
    beta_out_ref[...] = jnp.broadcast_to(sums, lanes)
    gamma_out_ref[...] = dots * (norms / divisor)
    dots_ref[...] = dots
    slopes = dots * gamma_ref[...] * (-norms / (divisor * divisor * units_all))

    @pl.when(pl.program_id(0) == 0)
    def _():
        slope_ref[...] = jnp.zeros_like(slope_ref)

    slope_ref[...] += jnp.sum(slopes[:, 0:1])


def back_pass(part, peer, target, live, w, hidden, scale, units_all, more=None, needed=()):
    tokens, channels = part.shape
    units = w.shape[0]
    block = 768
    lane, tiny, full = rows_at(block, LANES), whole((8, LANES)), whole((tokens, channels))
    in_specs = [full, full, full, whole((tokens, LANES)), rows_at(block, channels), rows_at(block, tokens)]
    out_specs = [full, rows_at(block, tokens), lane, lane]
    out_shape = [shape_of((tokens, channels), BF16), shape_of((units, tokens), BF16)]
    out_shape += [shape_of((units, LANES), F32)] * 2
    kernel = partial(back_first_kernel, scale=scale)
    if more is not None:
        kernel = partial(back_last_kernel, scale=scale, units_all=units_all)
        in_specs += [lane, lane, tiny, tiny, lane, lane]
        out_specs += [lane, tiny]
        out_shape += [shape_of((units, LANES), F32), shape_of((8, LANES), F32)]
    return call(
        kernel, units // block, in_specs, out_specs, out_shape, needed=needed,
    )(part, peer, target, live, w, hidden, *(more or ()))


def pre_grad_kernel(total_ref, peer_ref, slope_ref, peer_slope_ref, norms_ref, gamma_ref, dots_ref,
                    back_a, back_b, hidden_a, hidden_b, bend_a, bend_b, out_ref, *, units_all):
    divisor = (total_ref[0:1, :] + peer_ref[0:1, :]) / units_all + 1e-06
    d_total = slope_ref[0:1, :] + peer_slope_ref[0:1, :]
    norms = norms_ref[...]
    gamma = gamma_ref[...]
    ratio = norms / divisor
    along = gamma * ratio + 1.0
    across = (gamma * dots_ref[...] / divisor + d_total) / norms
    tokens = back_a.shape[1]
    for base, back, hidden, bend in ((0, back_a, hidden_a, bend_a), (tokens, back_b, hidden_b, bend_b)):
        for t in lane_tiles(tokens):
            value = (back[:, t].astype(F32) * along + across * hidden[:, t].astype(F32)) * bend[:, t].astype(F32)
            out_ref[:, base + t.start:base + t.stop] = value.astype(BF16)


def pre_grad(first, count, total, peer, slope, peer_slope, norms, gamma, dots, backs, hiddens, bends, units_all,
             needed=()):
    tokens = backs[0].shape[1]
    block = 256
    at = first // block
    lane, tiny, wide = rows_at(block, LANES, at), whole((8, LANES)), rows_at(block, tokens, at)
    return call(
        partial(pre_grad_kernel, units_all=units_all),
        count // block,
        [tiny] * 4 + [lane] * 3 + [wide] * 6,
        rows_at(block, 2 * tokens),
        shape_of((count, 2 * tokens), BF16),
        needed=needed,
    )(total, peer, slope, peer_slope, norms, gamma, dots, *backs, *hiddens, *bends)


def pair_kernel(own_ref, peer_ref, own_a, own_b, peer_a, peer_b, *refs):
    out_ref = refs[-1]
    tokens = own_a.shape[0]
    total = lax.dot_general(own_ref[:, :tokens], own_a[...], NN, preferred_element_type=F32)
    total += lax.dot_general(own_ref[:, tokens:], own_b[...], NN, preferred_element_type=F32)
    total += lax.dot_general(peer_ref[:, :tokens], peer_a[...], NN, preferred_element_type=F32)
    total += lax.dot_general(peer_ref[:, tokens:], peer_b[...], NN, preferred_element_type=F32)
    out_ref[...] = (total * 0.5).astype(BF16)


def pair_sum(first, units, own, peer, sides, filled=None, needed=()):
    count, tokens = own.shape
    channels = sides[0].shape[1]
    block = 256
    held = [] if filled is None else [filled]
    return call(
        pair_kernel,
        count // block,
        [rows_at(block, tokens)] * 2 + [whole((tokens // 2, channels))] * 4
        + [pl.BlockSpec(memory_space=pl.ANY)] * len(held),
        rows_at(block, channels, first // block),
        shape_of((units, channels), BF16),
        aliases={6: 0} if held else None,
        needed=needed,
    )(own, peer, *sides, *held)


def after(value, *needed):
    place = pl.BlockSpec(memory_space=pl.ANY)
    return pl.pallas_call(
        lambda *refs: None,
        in_specs=[place] * (1 + len(needed)),
        out_specs=place,
        out_shape=shape_of(value.shape, value.dtype),
        input_output_aliases={0: 0},
    )(value, *needed)


def pair_body(bit, pool, pick, token_mask, me, dw_kernel, dw_bias, ln_gain, ln_bias, w_in, grn_gamma, grn_beta, w_out):
    _, rows, cols, channels = pool.shape
    units = w_in.shape[0]
    units_all = 2 * units
    tokens = rows * cols
    scale = 1.0 / math.sqrt(2 * tokens)
    direct = bit == 0

    def across(value):
        return lax.ppermute(value, "shard", [(0, 1), (1, 0)])

    def to_peer(value):
        return lax.ppermute(value, "gossip", [(i, i ^ 1 << bit) for i in range(lax.axis_size("gossip"))])

    def live_of(keep):
        return jnp.broadcast_to((1.0 - keep.astype(F32))[..., None], (rows, cols, LANES))

    def cut(start, count):
        return lax.dynamic_slice(pool, (pick, start, 0, 0), (1, count, cols, channels))[0]

    near, far = rows // 2, rows - rows // 2 - 3
    upper = me == 0
    edge = cut(jnp.where(upper, rows - 3, 0), 3)
    edge_other = across(edge)
    mask_other = across(token_mask)
    mid_other = across(after(cut(jnp.where(upper, far, 3), near), edge_other))
    far_other = across(cut(jnp.where(upper, 0, 3 + near), far))
    sample = cut(0, rows)
    live, live_other = live_of(token_mask), live_of(mask_other)
    vectors = [dw_kernel.reshape(49, channels)] + [v.reshape(1, channels) for v in (dw_bias, ln_gain, ln_bias)]
    gamma, beta = columns(grn_gamma, grn_beta)
    me_vec = me.reshape(1)

    normed_own, = conv_norm(
        me_vec, (live, live_other), (sample, edge_other),
        ((None, 3, 0, 0), (0, rows, -rows, 3), (1, 3, 0, rows + 3)), None, vectors,
    )
    normed_other, = conv_norm(
        me_vec, (live, live_other), (edge, edge_other, mid_other),
        ((0, 3, -3, 0), (1, 3, 0, 3), (2, near, 3, 6)), 0, vectors, needed=(normed_own,),
    )
    normed_own = after(normed_own, normed_other)
    normed_own_p = to_peer(normed_own)
    hidden_own, bend_own, squares = expand(normed_own, w_in)
    normed_other, sample_other = conv_norm(
        me_vec, (live, live_other), (mid_other, far_other, edge_other),
        ((0, 6, 5, 0), (1, far, near + 3, 6), (None, 3, 0, far + 6)), 1, vectors,
        ((2, 0, rows - 3), (0, 3, far), (1, near + 3, 0)), (normed_other,), needed=(squares,),
    )
    hidden_other, bend_other, norms, total = expand(normed_other, w_in, squares)
    total_x = across(total)

    mixed, part_own, part_other = project(
        total, total_x, norms, gamma, beta, (hidden_own, hidden_other), w_out, units_all, needed=(normed_own_p,)
    )
    came_own = across(part_other)
    mixed_p = to_peer(mixed)
    came_other = across(part_own)

    errors_own, back_own, sums, dots = back_pass(
        part_own, came_own, sample.reshape(tokens, channels), live.reshape(tokens, LANES),
        w_out, hidden_own, scale, units_all,
    )
    errors_own_p = to_peer(errors_own)
    errors_other, back_other, g_beta, g_gamma, dots, slope = back_pass(
        part_other, came_other, sample_other.reshape(tokens, channels), live_other.reshape(tokens, LANES),
        w_out, hidden_other, scale, units_all, (sums, dots, total, total_x, norms, gamma),
    )
    slope_x = across(slope)
    if direct:
        normed_other_p = to_peer(after(normed_other, slope_x))
    else:
        normed_own_p = after(normed_own_p, slope_x)
        normed_other_p = across(normed_own_p)
    small = jnp.stack([g_gamma[:, 0], g_beta[:, 0]])
    small_p = to_peer(small)

    counts = (512, 512, units - 1024)
    firsts = (0, 512, 1024)
    gates = ((), (mixed_p,), ())
    pieces = []
    for first, count, gate in zip(firsts, counts, gates):
        own = pre_grad(
            first, count, total, total_x, slope, slope_x, norms, gamma, dots,
            (back_own, back_other), (hidden_own, hidden_other), (bend_own, bend_other), units_all,
            needed=gate + ((errors_own_p,) if first == firsts[2] else ()) + tuple(own for own, _ in pieces[-1:]),
        )
        pieces.append((own, to_peer(own)))
        if first == firsts[1]:
            if direct:
                errors_other_p = to_peer(after(errors_other, own))
            else:
                errors_own_p = after(errors_own_p, own)
                errors_other_p = across(errors_own_p)
    grad_out = pair_sum(0, units, mixed, mixed_p, (errors_own, errors_other, errors_own_p, errors_other_p))
    grad_in = None
    normed = (normed_own, normed_other, normed_own_p, normed_other_p)
    for first, (own, peer) in zip(firsts, pieces):
        gate = (grad_out,) if first == firsts[1] else ()
        grad_in = pair_sum(first, units, own, peer, normed, grad_in, needed=gate)
    small = (small + small_p) * 0.5
    return grad_in, grad_out, small[0], small[1]


def shortened(value):

    def short(part):
        return part.astype(jnp.bfloat16) if part.dtype == jnp.float32 else part

    return jax.tree.map(short, value)


def from_partner(value, axis, distance):
    return lax.ppermute(value, axis, [(i, i ^ 1 << distance) for i in range(lax.axis_size(axis))])


def with_halo(block, sides, width):
    for axis, dim in sides:
        count = lax.axis_size(axis)
        forward = [(i, i + 1) for i in range(count - 1)]
        backward = [(target, source) for source, target in forward]
        low = lax.ppermute(
            lax.slice_in_dim(block, block.shape[dim] - width, None, axis=dim), axis, forward
        )
        high = lax.ppermute(lax.slice_in_dim(block, 0, width, axis=dim), axis, backward)
        block = jnp.concatenate([low, block, high], axis=dim)
    return block


def depthwise(padded, kernel, bias_vec, height_rows, width_cols):
    result = jnp.zeros((height_rows, width_cols, kernel.shape[2]), jnp.float32)
    for i in range(7):
        for j in range(7):
            result = (
                result
                + padded[i : i + height_rows, j : j + width_cols].astype(jnp.float32) * kernel[i, j]
            )
    return result + bias_vec


def normalize(values, gain_vec, shift_vec):
    center = jnp.mean(values, axis=-1, keepdims=True)
    spread = jnp.mean(jnp.square(values - center), axis=-1, keepdims=True)
    return (values - center) * lax.rsqrt(spread + 1e-06) * gain_vec + shift_vec


def gelu_slope(pre_act):
    cdf_part = 0.5 * (1.0 + lax.erf(pre_act / math.sqrt(2.0)))
    pdf_part = jnp.exp(-0.5 * pre_act * pre_act) / math.sqrt(2.0 * math.pi)
    return cdf_part + pre_act * pdf_part


def peer_swap(payload, which_bit):
    return jax.tree.map(
        lambda part, own: part.astype(own.dtype),
        from_partner(shortened(payload), "gossip", which_bit),
        payload,
    )


def general_body(
    feature_pool,
    sample_ids,
    token_mask,
    step_index,
    dw_kernel,
    dw_bias,
    ln_gain,
    ln_bias,
    w_in,
    grn_gamma,
    grn_beta,
    w_out,
):
    levels = lax.axis_size("gossip").bit_length() - 1
    rotation = step_index[0] // levels
    pick = (sample_ids[0] + rotation) % POOL
    sample = lax.dynamic_index_in_dim(feature_pool[0], pick, 0, keepdims=False)
    keep = token_mask[0]
    local_rows, width_cols, channels = sample.shape
    w_in_local = w_in[0]
    w_out_local = w_out[0]
    gamma_vec = grn_gamma[0]
    beta_vec = grn_beta[0]
    error_scale = 1.0 / math.sqrt(H * W)
    masked = (sample.astype(jnp.float32) * (1.0 - keep.astype(jnp.float32))[..., None]).astype(
        jnp.bfloat16
    )
    rimmed = with_halo(masked, (("shard", 0),), 3)
    padded = jnp.pad(rimmed, ((0, 0), (3, 3), (0, 0)))
    normed = (
        normalize(depthwise(padded, dw_kernel, dw_bias, local_rows, width_cols), ln_gain, ln_bias)
        .astype(jnp.bfloat16)
        .reshape(-1, channels)
    )
    gathered = lax.all_gather(normed, "shard", axis=0, tiled=True)
    pre_act = lax.dot_general(
        gathered, w_in_local, (((1,), (1,)), ((), ())), preferred_element_type=jnp.float32
    )
    hidden = jax.nn.gelu(pre_act, approximate=False)
    norms = jnp.sqrt(jnp.sum(hidden * hidden, axis=0) + 1e-06)
    norm_total = lax.psum(jnp.sum(norms), "shard")
    divisor = norm_total / HID + 1e-06
    ratio = norms / divisor
    mixed = (gamma_vec * (hidden * ratio) + beta_vec + hidden).astype(jnp.bfloat16)
    own_sum = lax.psum_scatter(
        jnp.dot(mixed, w_out_local, preferred_element_type=jnp.float32).astype(jnp.bfloat16),
        "shard",
        scatter_dimension=0,
        tiled=True,
    ).astype(jnp.float32)
    output_own = masked.astype(jnp.float32).reshape(-1, channels) + own_sum
    target_own = sample.astype(jnp.float32).reshape(-1, channels)
    errors_own = (
        keep.astype(jnp.float32).reshape(-1, 1) * (output_own - target_own) * error_scale
    ).astype(jnp.bfloat16)
    errors_all = lax.all_gather(errors_own, "shard", axis=0, tiled=True)
    grad_out_local = lax.dot_general(
        mixed, errors_all, (((0,), (0,)), ((), ())), preferred_element_type=jnp.float32
    )
    back = lax.dot_general(
        errors_all, w_out_local, (((1,), (1,)), ((), ())), preferred_element_type=jnp.float32
    )
    grad_gamma_local = jnp.sum(back * hidden * ratio, axis=0)
    grad_beta_local = jnp.sum(back, axis=0)
    d_ratio = jnp.sum(back * gamma_vec * hidden, axis=0)
    slope_local = jnp.sum(d_ratio * (-norms / (divisor * divisor * HID)))
    d_total = lax.psum(slope_local, "shard")
    d_norms = d_ratio / divisor + d_total
    d_hidden = back * (gamma_vec * ratio + 1.0) + d_norms / norms * hidden
    d_pre = (d_hidden * gelu_slope(pre_act)).astype(jnp.bfloat16)
    grad_in_local = lax.dot_general(
        d_pre, gathered, (((0,), (0,)), ((), ())), preferred_element_type=jnp.float32
    )
    own_grads = (grad_in_local, grad_out_local, grad_gamma_local, grad_beta_local)
    branches = [partial(peer_swap, which_bit=b) for b in range(levels)]
    peer_grads = lax.switch(step_index[0] % levels, branches, own_grads)
    grad_in = ((own_grads[0] + peer_grads[0]) * 0.5).astype(jnp.bfloat16)
    grad_out = ((own_grads[1] + peer_grads[1]) * 0.5).astype(jnp.bfloat16)
    grad_gamma = (own_grads[2] + peer_grads[2]) * 0.5
    grad_beta = (own_grads[3] + peer_grads[3]) * 0.5
    return (grad_in[None], grad_out[None], grad_gamma[None], grad_beta[None])


def body(
    feature_pool,
    sample_ids,
    token_mask,
    step_index,
    dw_kernel,
    dw_bias,
    ln_gain,
    ln_bias,
    w_in,
    grn_gamma,
    grn_beta,
    w_out,
):
    if lax.axis_size("shard") != 2:
        return general_body(
            feature_pool, sample_ids, token_mask, step_index, dw_kernel, dw_bias,
            ln_gain, ln_bias, w_in, grn_gamma, grn_beta, w_out,
        )
    levels = lax.axis_size("gossip").bit_length() - 1
    pick = (sample_ids[0] + step_index[0] // levels) % feature_pool.shape[1]
    me = lax.axis_index("shard").astype(jnp.int32)
    outs = lax.switch(
        step_index[0] % levels,
        [partial(pair_body, bit) for bit in range(levels)],
        feature_pool[0], pick, token_mask[0], me, dw_kernel, dw_bias, ln_gain, ln_bias,
        w_in[0], grn_gamma[0], grn_beta[0], w_out[0],
    )
    return tuple(out[None] for out in outs)


def solution(mesh):
    in_specs = (
        P("gossip", None, "shard", None, None),
        P("gossip"),
        P("gossip", "shard", None),
        P(),
        P(),
        P(),
        P(),
        P(),
        P("gossip", "shard", None),
        P("gossip", "shard"),
        P("gossip", "shard"),
        P("gossip", "shard", None),
    )
    out_specs = (
        P("gossip", "shard", None),
        P("gossip", "shard", None),
        P("gossip", "shard"),
        P("gossip", "shard"),
    )
    return jax.shard_map(body, mesh=mesh, in_specs=in_specs, out_specs=out_specs, check_vma=False)
```

```python
from functools import partial
import math

import jax
import jax.numpy as jnp
from jax import lax
from jax.experimental import pallas as pl
from jax.experimental.pallas import tpu as pltpu
from jax.sharding import PartitionSpec as P

HID = 3072
H = 32
W = 32
POOL = 2
LANES = 128
F32 = jnp.float32
BF16 = jnp.bfloat16
NT = (((1,), (1,)), ((), ()))
TN = (((0,), (0,)), ((), ()))
NN = (((1,), (0,)), ((), ()))


def shape_of(dims, dtype):
    return jax.ShapeDtypeStruct(dims, dtype)


def whole(dims):
    return pl.BlockSpec(dims, lambda i: (0,) * len(dims))


def rows_at(block, width, offset=0):
    return pl.BlockSpec((block, width), lambda i: (i + offset, 0))


def call(kernel, grid, in_specs, out_specs, out_shape, scratch=(), aliases=None, needed=()):
    inputs, extra = len(in_specs), len(needed)

    def run(*refs):
        kernel(*refs[:inputs], *refs[inputs + extra:])

    def placed(shape):
        return pltpu.HBM(shape.shape, shape.dtype) if math.prod(shape.shape) > 1 << 16 else shape

    single = not isinstance(out_shape, list)
    held = placed(out_shape) if single else [placed(s) for s in out_shape]
    built = pl.pallas_call(
        run,
        grid=(grid,),
        in_specs=list(in_specs) + [pl.BlockSpec(memory_space=pl.ANY)] * extra,
        out_specs=out_specs,
        out_shape=held,
        scratch_shapes=list(scratch),
        input_output_aliases=aliases or {},
        compiler_params=pltpu.CompilerParams(
            dimension_semantics=("arbitrary",), vmem_limit_bytes=48 * 1024 * 1024
        ),
    )
    def in_hbm(value):
        return pltpu.with_memory_space_constraint(value, pltpu.HBM) if value.size > 1 << 16 else value

    return lambda *args: built(*map(in_hbm, args), *map(in_hbm, needed))


def lane_tiles(width):
    return [slice(k * LANES, (k + 1) * LANES) for k in range(width // LANES)]


def folded(value):
    tiles = [value[:, t] for t in lane_tiles(value.shape[1])]
    return sum(tiles[1:], tiles[0])


def conv_kernel(me_ref, live_own_ref, live_other_ref, tap_ref, bias_ref, gain_ref, shift_ref, *refs,
                parts, out_rows, half, copies, held):
    scratch = 4 + bool(copies)
    outs = 1 + bool(copies)
    sources = refs[:len(refs) - scratch - outs - held]
    out_ref = refs[-scratch - outs]
    pad_ref, conv_ref, norm_ref, sems = refs[-scratch:len(refs) - scratch + 4]
    rows, cols, _ = live_own_ref.shape
    blocks = conv_ref.shape[0]
    window = out_rows + 6
    upper = me_ref[0] == 0
    inner = slice(8, 8 + cols)
    moves = []
    if copies:
        map_ref, map_sems = refs[-scratch - 1], refs[-1]
        for n, (source, at, mirrored) in enumerate(copies):
            there = pl.ds(jnp.where(upper, at, mirrored), sources[source].shape[0])
            moves.append(pltpu.make_async_copy(sources[source], map_ref.at[there], map_sems.at[n]))
            moves[-1].start()
    pad_ref[:, 0:8, :] = jnp.zeros((window, 8, LANES), F32)
    pad_ref[:, 8 + cols:, :] = jnp.zeros((window, 8, LANES), F32)
    group = 8

    def one_block(c, carry):
        lane = pl.ds(pl.multiple_of(c * LANES, LANES), LANES)
        for source, count, distance, place in parts:
            there = pl.ds(jnp.where(upper, place, window - count - place), count)
            if source is None:
                pad_ref[there, inner, :] = jnp.zeros((count, cols, LANES), F32)
                continue
            own = distance < 0
            live_ref = live_own_ref if own else live_other_ref
            first = jnp.where(upper, distance + rows if own else distance,
                              -distance - count if own else rows - distance - count)
            length = sources[source].shape[0]
            values = sources[source][pl.ds(jnp.where(upper, length - count, 0), count), :, lane]
            pad_ref[there, inner, :] = values.astype(F32) * live_ref[pl.ds(first, count)]

        def one_group(g, carry):
            base = g * group
            acc = [jnp.broadcast_to(bias_ref[:, lane], (cols, LANES)) for _ in range(group)]
            for j in range(7):
                for q in range(group + 6):
                    x = pad_ref[base + q, 5 + j:5 + j + cols, :]
                    for r in range(max(0, q - 6), min(group, q + 1)):
                        tap = (q - r) * 7 + j
                        acc[r] = acc[r] + x * tap_ref[tap:tap + 1, lane]
            for r in range(group):
                conv_ref[c, pl.ds((base + r) * cols, cols), :] = acc[r]
            return carry

        return lax.fori_loop(0, out_rows // group, one_group, carry, unroll=True)

    lax.fori_loop(0, blocks, one_block, 0)
    step = 32
    channels = blocks * LANES
    base = 0
    if half is not None:
        base = jnp.where(upper, half, 1 - half) * (out_rows * cols)

    def one_step(t, carry):
        here = pl.ds(pl.multiple_of(t * step, step), step)
        values = [conv_ref[k, here, :] for k in range(blocks)]
        center = jnp.sum(sum(values[1:], values[0]), axis=1, keepdims=True) / channels
        away = [v - center for v in values]
        squares = [d * d for d in away]
        spread = jnp.sum(sum(squares[1:], squares[0]), axis=1, keepdims=True) / channels
        inverse = lax.rsqrt(spread + 1e-06)
        for k, t_k in enumerate(lane_tiles(channels)):
            norm_ref[here, t_k] = (away[k] * inverse * gain_ref[:, t_k] + shift_ref[:, t_k]).astype(BF16)
        return carry

    quarter = out_rows * cols // 4
    for n in range(4):
        lax.fori_loop(n * quarter // step, (n + 1) * quarter // step, one_step, 0, unroll=True)
        there = pl.ds(pl.multiple_of(base + n * quarter, quarter), quarter)
        moves.append(pltpu.make_async_copy(norm_ref.at[n * quarter:(n + 1) * quarter], out_ref.at[there], sems.at[n]))
        moves[-1].start()
    for move in moves:
        move.wait()


def conv_norm(me, lives, maps, parts, half, vectors, copies=(), filled=(), needed=()):
    rows, cols = lives[0].shape[:2]
    channels = vectors[0].shape[1]
    blocks = channels // LANES
    out_rows = rows if half is None else rows // 2
    inputs = 7 + len(maps)
    held = len(filled)
    place = pl.BlockSpec(memory_space=pltpu.HBM)
    more = bool(copies)
    return call(
        partial(conv_kernel, parts=parts, out_rows=out_rows, half=half, copies=copies, held=held),
        1,
        [pl.BlockSpec(memory_space=pltpu.SMEM)]
        + [whole(v.shape) for v in (*lives, *vectors, *maps)]
        + [pl.BlockSpec(memory_space=pl.ANY)] * held,
        [place] * (1 + more),
        [shape_of((rows * cols, channels), BF16)] + [shape_of((rows, cols, channels), BF16)] * more,
        [
            pltpu.VMEM((out_rows + 6, cols + 16, LANES), F32),
            pltpu.VMEM((blocks, out_rows * cols, LANES), F32),
            pltpu.VMEM((out_rows * cols, channels), BF16),
            pltpu.SemaphoreType.DMA((4,)),
        ] + [pltpu.SemaphoreType.DMA((len(copies),))] * more,
        aliases={inputs: 0} if held else None,
        needed=needed,
    )(me, *lives, *vectors, *maps, *filled)


def columns_kernel(gamma_ref, beta_ref, gamma_out, beta_out):
    for row, out in ((gamma_ref, gamma_out), (beta_ref, beta_out)):
        out[...] = jnp.broadcast_to(row[...], (LANES, row.shape[1])).T


def columns(gamma, beta):
    units = gamma.shape[0]
    return call(
        columns_kernel, 1, [whole((1, units))] * 2, [whole((units, LANES))] * 2,
        [shape_of((units, LANES), F32)] * 2,
    )(gamma[None], beta[None])


def expand_block(normed_ref, w_ref, hidden_ref, slope_ref):
    pre_act = lax.dot_general(w_ref[...], normed_ref[...], NT, preferred_element_type=F32)
    cdf = 0.5 * (1.0 + lax.erf(pre_act * math.sqrt(0.5)))
    hidden = pre_act * cdf
    hidden_ref[...] = hidden.astype(BF16)
    slope = cdf + pre_act * (jnp.exp(-0.5 * pre_act * pre_act) * (1.0 / math.sqrt(2.0 * math.pi)))
    slope_ref[...] = slope.astype(BF16)
    return folded(hidden * hidden)


def expand_first_kernel(normed_ref, w_ref, hidden_ref, slope_ref, square_ref):
    square_ref[...] = expand_block(normed_ref, w_ref, hidden_ref, slope_ref)


def expand_last_kernel(normed_ref, w_ref, before_ref, hidden_ref, slope_ref, norms_ref, total_ref):
    square = expand_block(normed_ref, w_ref, hidden_ref, slope_ref) + before_ref[...]
    norms = jnp.sqrt(jnp.sum(square, axis=1, keepdims=True) + 1e-06)
    norms_ref[...] = jnp.broadcast_to(norms, norms_ref.shape)

    @pl.when(pl.program_id(0) == 0)
    def _():
        total_ref[...] = jnp.zeros_like(total_ref)

    total_ref[...] += jnp.sum(norms)


def expand(normed, w, before=None, needed=()):
    tokens, channels = normed.shape
    units = w.shape[0]
    block = 512
    last = before is not None
    wide, lane = rows_at(block, tokens), rows_at(block, LANES)
    out_specs = [wide, wide, lane] + [whole((8, LANES))] * last
    out_shape = [shape_of((units, tokens), BF16)] * 2 + [shape_of((units, LANES), F32)]
    out_shape += [shape_of((8, LANES), F32)] * last
    return call(
        expand_last_kernel if last else expand_first_kernel,
        units // block,
        [whole((tokens, channels)), rows_at(block, channels)] + [lane] * last,
        out_specs,
        out_shape,
        needed=needed,
    )(normed, w, *([before] if last else []))


def project_kernel(total_ref, peer_ref, norms_ref, gamma_ref, beta_ref, hidden_own_ref, hidden_other_ref, w_ref,
                   mixed_ref, part_own_ref, part_other_ref, acc_ref, *, steps, units_all):
    k = pl.program_id(0)
    divisor = (total_ref[0:1, :] + peer_ref[0:1, :]) / units_all + 1e-06
    scale = gamma_ref[...] * (norms_ref[...] / divisor) + 1.0
    shift = beta_ref[...]
    tokens = hidden_own_ref.shape[1]
    for base, hidden_ref in ((0, hidden_own_ref), (tokens, hidden_other_ref)):
        for t in lane_tiles(tokens):
            value = hidden_ref[:, t].astype(F32) * scale + shift
            mixed_ref[:, base + t.start:base + t.stop] = value.astype(BF16)
    for n, part_ref in ((0, part_own_ref), (1, part_other_ref)):
        product = lax.dot_general(
            mixed_ref[:, n * tokens:(n + 1) * tokens], w_ref[...], TN, preferred_element_type=F32
        )

        @pl.when(k == 0)
        def _():
            acc_ref[n] = product

        @pl.when((k > 0) & (k < steps - 1))
        def _():
            acc_ref[n] += product

        @pl.when(k == steps - 1)
        def _():
            part_ref[...] = (acc_ref[n] + product).astype(BF16)


def project(total, peer, norms, gamma, beta, hiddens, w, units_all, needed=()):
    units, tokens = hiddens[0].shape
    channels = w.shape[1]
    block = 512
    lane, tiny, part = rows_at(block, LANES), whole((8, LANES)), whole((tokens, channels))
    return call(
        partial(project_kernel, steps=units // block, units_all=units_all),
        units // block,
        [tiny, tiny, lane, lane, lane, rows_at(block, tokens), rows_at(block, tokens), rows_at(block, channels)],
        [rows_at(block, 2 * tokens), part, part],
        [shape_of((units, 2 * tokens), BF16)] + [shape_of((tokens, channels), BF16)] * 2,
        [pltpu.VMEM((2, tokens, channels), F32)],
        needed=needed,
    )(total, peer, norms, gamma, beta, *hiddens, w)


def back_block(part_ref, peer_ref, target_ref, live_ref, w_ref, hidden_ref, errors_ref, back_ref, scale):
    @pl.when(pl.program_id(0) == 0)
    def _():
        live = live_ref[...]
        keep = (1.0 - live) * scale
        for t in lane_tiles(target_ref.shape[1]):
            target = target_ref[:, t].astype(F32)
            summed = part_ref[:, t].astype(F32) + peer_ref[:, t].astype(F32)
            errors_ref[:, t] = (keep * (target * live + summed - target)).astype(BF16)

    back = lax.dot_general(w_ref[...], errors_ref[...], NT, preferred_element_type=F32)
    back_ref[...] = back.astype(BF16)
    return folded(back), folded(back * hidden_ref[...].astype(F32))


def back_first_kernel(part_ref, peer_ref, target_ref, live_ref, w_ref, hidden_ref,
                      errors_ref, back_ref, sum_ref, dot_ref, *, scale):
    sum_ref[...], dot_ref[...] = back_block(
        part_ref, peer_ref, target_ref, live_ref, w_ref, hidden_ref, errors_ref, back_ref, scale
    )


def back_last_kernel(part_ref, peer_ref, target_ref, live_ref, w_ref, hidden_ref,
                     sum_before_ref, dot_before_ref, total_ref, peer_total_ref, norms_ref, gamma_ref,
                     errors_ref, back_ref, beta_out_ref, gamma_out_ref, dots_ref, slope_ref, *, scale, units_all):
    sums, dots = back_block(
        part_ref, peer_ref, target_ref, live_ref, w_ref, hidden_ref, errors_ref, back_ref, scale
    )
    lanes = beta_out_ref.shape
    sums = jnp.sum(sums + sum_before_ref[...], axis=1, keepdims=True)
    dots = jnp.broadcast_to(jnp.sum(dots + dot_before_ref[...], axis=1, keepdims=True), lanes)
    divisor = (total_ref[0:1, :] + peer_total_ref[0:1, :]) / units_all + 1e-06
    norms = norms_ref[...]
    beta_out_ref[...] = jnp.broadcast_to(sums, lanes)
    gamma_out_ref[...] = dots * (norms / divisor)
    dots_ref[...] = dots
    slopes = dots * gamma_ref[...] * (-norms / (divisor * divisor * units_all))

    @pl.when(pl.program_id(0) == 0)
    def _():
        slope_ref[...] = jnp.zeros_like(slope_ref)

    slope_ref[...] += jnp.sum(slopes[:, 0:1])


def back_pass(part, peer, target, live, w, hidden, scale, units_all, more=None, needed=()):
    tokens, channels = part.shape
    units = w.shape[0]
    block = 768
    lane, tiny, full = rows_at(block, LANES), whole((8, LANES)), whole((tokens, channels))
    in_specs = [full, full, full, whole((tokens, LANES)), rows_at(block, channels), rows_at(block, tokens)]
    out_specs = [full, rows_at(block, tokens), lane, lane]
    out_shape = [shape_of((tokens, channels), BF16), shape_of((units, tokens), BF16)]
    out_shape += [shape_of((units, LANES), F32)] * 2
    kernel = partial(back_first_kernel, scale=scale)
    if more is not None:
        kernel = partial(back_last_kernel, scale=scale, units_all=units_all)
        in_specs += [lane, lane, tiny, tiny, lane, lane]
        out_specs += [lane, tiny]
        out_shape += [shape_of((units, LANES), F32), shape_of((8, LANES), F32)]
    return call(
        kernel, units // block, in_specs, out_specs, out_shape, needed=needed,
    )(part, peer, target, live, w, hidden, *(more or ()))


def pre_grad_kernel(total_ref, peer_ref, slope_ref, peer_slope_ref, norms_ref, gamma_ref, dots_ref,
                    back_a, back_b, hidden_a, hidden_b, bend_a, bend_b, out_ref, *, units_all):
    divisor = (total_ref[0:1, :] + peer_ref[0:1, :]) / units_all + 1e-06
    d_total = slope_ref[0:1, :] + peer_slope_ref[0:1, :]
    norms = norms_ref[...]
    gamma = gamma_ref[...]
    ratio = norms / divisor
    along = gamma * ratio + 1.0
    across = (gamma * dots_ref[...] / divisor + d_total) / norms
    tokens = back_a.shape[1]
    for base, back, hidden, bend in ((0, back_a, hidden_a, bend_a), (tokens, back_b, hidden_b, bend_b)):
        for t in lane_tiles(tokens):
            value = (back[:, t].astype(F32) * along + across * hidden[:, t].astype(F32)) * bend[:, t].astype(F32)
            out_ref[:, base + t.start:base + t.stop] = value.astype(BF16)


def pre_grad(first, count, total, peer, slope, peer_slope, norms, gamma, dots, backs, hiddens, bends, units_all,
             needed=()):
    tokens = backs[0].shape[1]
    block = 256
    at = first // block
    lane, tiny, wide = rows_at(block, LANES, at), whole((8, LANES)), rows_at(block, tokens, at)
    return call(
        partial(pre_grad_kernel, units_all=units_all),
        count // block,
        [tiny] * 4 + [lane] * 3 + [wide] * 6,
        rows_at(block, 2 * tokens),
        shape_of((count, 2 * tokens), BF16),
        needed=needed,
    )(total, peer, slope, peer_slope, norms, gamma, dots, *backs, *hiddens, *bends)


def pair_kernel(*refs, terms, carried, final):
    out_ref = refs[-1]
    total = refs[2 * terms][...] if carried else None
    for n in range(terms):
        product = lax.dot_general(refs[n][...], refs[terms + n][...], NN, preferred_element_type=F32)
        total = product if total is None else total + product
    out_ref[...] = (total * 0.5).astype(BF16) if final else total


def pair_sum(terms, first=0, units=None, carried=None, final=True, filled=None, needed=()):
    count = terms[0][0].shape[0]
    tokens, channels = terms[0][2].shape
    units = units or count
    block = 256
    sums = [] if carried is None else [carried]
    held = [] if filled is None else [filled]
    inputs = 2 * len(terms) + len(sums)

    def left(half):
        return pl.BlockSpec((block, tokens), lambda i: (i, half))

    return call(
        partial(pair_kernel, terms=len(terms), carried=bool(sums), final=final),
        count // block,
        [left(half) for _, half, _ in terms] + [whole((tokens, channels))] * len(terms)
        + [rows_at(block, channels)] * len(sums)
        + [pl.BlockSpec(memory_space=pl.ANY)] * len(held),
        rows_at(block, channels, first // block),
        shape_of((units, channels), BF16 if final else F32),
        aliases={inputs: 0} if held else None,
        needed=needed,
    )(*[t[0] for t in terms], *[t[2] for t in terms], *sums, *held)


def after(value, *needed):
    place = pl.BlockSpec(memory_space=pl.ANY)
    return pl.pallas_call(
        lambda *refs: None,
        in_specs=[place] * (1 + len(needed)),
        out_specs=place,
        out_shape=shape_of(value.shape, value.dtype),
        input_output_aliases={0: 0},
    )(value, *needed)


def pair_body(bit, pool, pick, token_mask, me, dw_kernel, dw_bias, ln_gain, ln_bias, w_in, grn_gamma, grn_beta, w_out):
    _, rows, cols, channels = pool.shape
    units = w_in.shape[0]
    units_all = 2 * units
    tokens = rows * cols
    scale = 1.0 / math.sqrt(2 * tokens)
    direct = bit == 0

    def across(value):
        return lax.ppermute(value, "shard", [(0, 1), (1, 0)])

    def to_peer(value):
        return lax.ppermute(value, "gossip", [(i, i ^ 1 << bit) for i in range(lax.axis_size("gossip"))])

    def live_of(keep):
        return jnp.broadcast_to((1.0 - keep.astype(F32))[..., None], (rows, cols, LANES))

    def cut(start, count):
        return lax.dynamic_slice(pool, (pick, start, 0, 0), (1, count, cols, channels))[0]

    near, far = rows // 2, rows - rows // 2 - 3
    upper = me == 0
    edge = cut(jnp.where(upper, rows - 3, 0), 3)
    edge_other = across(edge)
    mask_other = across(token_mask)
    sample = cut(0, rows)
    taps = dw_kernel.reshape(49, channels)
    mid_other = across(after(cut(jnp.where(upper, far, 3), near), edge_other, mask_other, sample, taps))
    far_other = across(cut(jnp.where(upper, 0, 3 + near), far))
    live, live_other = live_of(token_mask), live_of(mask_other)
    vectors = [taps] + [v.reshape(1, channels) for v in (dw_bias, ln_gain, ln_bias)]
    gamma, beta = columns(grn_gamma, grn_beta)
    me_vec = me.reshape(1)

    normed_own, = conv_norm(
        me_vec, (live, live_other), (sample, edge_other),
        ((None, 3, 0, 0), (0, rows, -rows, 3), (1, 3, 0, rows + 3)), None, vectors,
    )
    normed_other, = conv_norm(
        me_vec, (live, live_other), (edge, edge_other, mid_other),
        ((0, 3, -3, 0), (1, 3, 0, 3), (2, near, 3, 6)), 0, vectors, needed=(normed_own,),
    )
    normed_own = after(normed_own, normed_other)
    normed_own_p = to_peer(normed_own)
    hidden_own, bend_own, squares = expand(normed_own, w_in)
    normed_other, sample_other = conv_norm(
        me_vec, (live, live_other), (mid_other, far_other, edge_other),
        ((0, 6, 5, 0), (1, far, near + 3, 6), (None, 3, 0, far + 6)), 1, vectors,
        ((2, 0, rows - 3), (0, 3, far), (1, near + 3, 0)), (normed_other,), needed=(squares,),
    )
    hidden_other, bend_other, norms, total = expand(normed_other, w_in, squares)
    total_x = across(total)

    mixed, part_own, part_other = project(
        total, total_x, norms, gamma, beta, (hidden_own, hidden_other), w_out, units_all, needed=(normed_own_p,)
    )
    came_own = across(part_other)
    mixed_p = to_peer(mixed)
    came_other = across(part_own)

    errors_own, back_own, sums, dots = back_pass(
        part_own, came_own, sample.reshape(tokens, channels), live.reshape(tokens, LANES),
        w_out, hidden_own, scale, units_all,
    )
    errors_own_p = to_peer(errors_own)
    errors_other, back_other, g_beta, g_gamma, dots, slope = back_pass(
        part_other, came_other, sample_other.reshape(tokens, channels), live_other.reshape(tokens, LANES),
        w_out, hidden_other, scale, units_all, (sums, dots, total, total_x, norms, gamma),
    )
    small = jnp.stack([g_gamma[:, 0], g_beta[:, 0]])
    slope_x = across(slope)
    if direct:
        normed_other_p = to_peer(normed_other)
        errors_other_p = to_peer(errors_other)
        counts = (units,)
    else:
        normed_own_p = after(normed_own_p, slope_x)
        normed_other_p = across(normed_own_p)
        counts = (units // 2, units // 3, units // 6)
    small_p = to_peer(small)

    pieces, sums = [], []
    first = 0
    for n, count in enumerate(counts):
        own = pre_grad(
            first, count, total, total_x, slope, slope_x, norms, gamma, dots,
            (back_own, back_other), (hidden_own, hidden_other), (bend_own, bend_other), units_all,
            needed=tuple(own for _, own, _ in pieces[-1:]) + ((mixed_p,) if n == 1 else ()) + ((normed_other_p,) if n == 2 else ()),
        )
        pieces.append((first, own, to_peer(own)))
        if not direct:
            sums.append(pair_sum(((own, 0, normed_own), (own, 1, normed_other)), final=False))
        first += count
        if not direct and n == 1:
            errors_own_p = after(errors_own_p, own, *sums)
            errors_other_p = across(errors_own_p)
            early = pair_sum(((mixed, 0, errors_own), (mixed_p, 0, errors_own_p)), final=False)
    out_terms = ((mixed, 1, errors_other), (mixed_p, 1, errors_other_p))
    if direct:
        out_terms += ((mixed, 0, errors_own), (mixed_p, 0, errors_own_p))
    grad_out = pair_sum(out_terms, carried=None if direct else early)
    grad_in = None
    for n, (first, own, peer) in enumerate(pieces):
        own_terms = ((own, 0, normed_own), (own, 1, normed_other))
        peer_terms = ((peer, 0, normed_own_p), (peer, 1, normed_other_p))
        gate = (grad_out,) if n == (0 if direct else 1) else ()
        if direct:
            grad_in = pair_sum(own_terms + peer_terms, first, units, None, True, grad_in, gate)
            continue
        if n == 0:
            gate = (early, *sums[1:])
        grad_in = pair_sum(peer_terms, first, units, sums[n], True, grad_in, gate)
        if n == 1:
            small_p = after(small_p, grad_in)
    small = (small + small_p) * 0.5
    return grad_in, grad_out, small[0], small[1]


def shortened(value):

    def short(part):
        return part.astype(jnp.bfloat16) if part.dtype == jnp.float32 else part

    return jax.tree.map(short, value)


def from_partner(value, axis, distance):
    return lax.ppermute(value, axis, [(i, i ^ 1 << distance) for i in range(lax.axis_size(axis))])


def with_halo(block, sides, width):
    for axis, dim in sides:
        count = lax.axis_size(axis)
        forward = [(i, i + 1) for i in range(count - 1)]
        backward = [(target, source) for source, target in forward]
        low = lax.ppermute(
            lax.slice_in_dim(block, block.shape[dim] - width, None, axis=dim), axis, forward
        )
        high = lax.ppermute(lax.slice_in_dim(block, 0, width, axis=dim), axis, backward)
        block = jnp.concatenate([low, block, high], axis=dim)
    return block


def depthwise(padded, kernel, bias_vec, height_rows, width_cols):
    result = jnp.zeros((height_rows, width_cols, kernel.shape[2]), jnp.float32)
    for i in range(7):
        for j in range(7):
            result = (
                result
                + padded[i : i + height_rows, j : j + width_cols].astype(jnp.float32) * kernel[i, j]
            )
    return result + bias_vec


def normalize(values, gain_vec, shift_vec):
    center = jnp.mean(values, axis=-1, keepdims=True)
    spread = jnp.mean(jnp.square(values - center), axis=-1, keepdims=True)
    return (values - center) * lax.rsqrt(spread + 1e-06) * gain_vec + shift_vec


def gelu_slope(pre_act):
    cdf_part = 0.5 * (1.0 + lax.erf(pre_act / math.sqrt(2.0)))
    pdf_part = jnp.exp(-0.5 * pre_act * pre_act) / math.sqrt(2.0 * math.pi)
    return cdf_part + pre_act * pdf_part


def peer_swap(payload, which_bit):
    return jax.tree.map(
        lambda part, own: part.astype(own.dtype),
        from_partner(shortened(payload), "gossip", which_bit),
        payload,
    )


def general_body(
    feature_pool,
    sample_ids,
    token_mask,
    step_index,
    dw_kernel,
    dw_bias,
    ln_gain,
    ln_bias,
    w_in,
    grn_gamma,
    grn_beta,
    w_out,
):
    levels = lax.axis_size("gossip").bit_length() - 1
    rotation = step_index[0] // levels
    pick = (sample_ids[0] + rotation) % POOL
    sample = lax.dynamic_index_in_dim(feature_pool[0], pick, 0, keepdims=False)
    keep = token_mask[0]
    local_rows, width_cols, channels = sample.shape
    w_in_local = w_in[0]
    w_out_local = w_out[0]
    gamma_vec = grn_gamma[0]
    beta_vec = grn_beta[0]
    error_scale = 1.0 / math.sqrt(H * W)
    masked = (sample.astype(jnp.float32) * (1.0 - keep.astype(jnp.float32))[..., None]).astype(
        jnp.bfloat16
    )
    rimmed = with_halo(masked, (("shard", 0),), 3)
    padded = jnp.pad(rimmed, ((0, 0), (3, 3), (0, 0)))
    normed = (
        normalize(depthwise(padded, dw_kernel, dw_bias, local_rows, width_cols), ln_gain, ln_bias)
        .astype(jnp.bfloat16)
        .reshape(-1, channels)
    )
    gathered = lax.all_gather(normed, "shard", axis=0, tiled=True)
    pre_act = lax.dot_general(
        gathered, w_in_local, (((1,), (1,)), ((), ())), preferred_element_type=jnp.float32
    )
    hidden = jax.nn.gelu(pre_act, approximate=False)
    norms = jnp.sqrt(jnp.sum(hidden * hidden, axis=0) + 1e-06)
    norm_total = lax.psum(jnp.sum(norms), "shard")
    divisor = norm_total / HID + 1e-06
    ratio = norms / divisor
    mixed = (gamma_vec * (hidden * ratio) + beta_vec + hidden).astype(jnp.bfloat16)
    own_sum = lax.psum_scatter(
        jnp.dot(mixed, w_out_local, preferred_element_type=jnp.float32).astype(jnp.bfloat16),
        "shard",
        scatter_dimension=0,
        tiled=True,
    ).astype(jnp.float32)
    output_own = masked.astype(jnp.float32).reshape(-1, channels) + own_sum
    target_own = sample.astype(jnp.float32).reshape(-1, channels)
    errors_own = (
        keep.astype(jnp.float32).reshape(-1, 1) * (output_own - target_own) * error_scale
    ).astype(jnp.bfloat16)
    errors_all = lax.all_gather(errors_own, "shard", axis=0, tiled=True)
    grad_out_local = lax.dot_general(
        mixed, errors_all, (((0,), (0,)), ((), ())), preferred_element_type=jnp.float32
    )
    back = lax.dot_general(
        errors_all, w_out_local, (((1,), (1,)), ((), ())), preferred_element_type=jnp.float32
    )
    grad_gamma_local = jnp.sum(back * hidden * ratio, axis=0)
    grad_beta_local = jnp.sum(back, axis=0)
    d_ratio = jnp.sum(back * gamma_vec * hidden, axis=0)
    slope_local = jnp.sum(d_ratio * (-norms / (divisor * divisor * HID)))
    d_total = lax.psum(slope_local, "shard")
    d_norms = d_ratio / divisor + d_total
    d_hidden = back * (gamma_vec * ratio + 1.0) + d_norms / norms * hidden
    d_pre = (d_hidden * gelu_slope(pre_act)).astype(jnp.bfloat16)
    grad_in_local = lax.dot_general(
        d_pre, gathered, (((0,), (0,)), ((), ())), preferred_element_type=jnp.float32
    )
    own_grads = (grad_in_local, grad_out_local, grad_gamma_local, grad_beta_local)
    branches = [partial(peer_swap, which_bit=b) for b in range(levels)]
    peer_grads = lax.switch(step_index[0] % levels, branches, own_grads)
    grad_in = ((own_grads[0] + peer_grads[0]) * 0.5).astype(jnp.bfloat16)
    grad_out = ((own_grads[1] + peer_grads[1]) * 0.5).astype(jnp.bfloat16)
    grad_gamma = (own_grads[2] + peer_grads[2]) * 0.5
    grad_beta = (own_grads[3] + peer_grads[3]) * 0.5
    return (grad_in[None], grad_out[None], grad_gamma[None], grad_beta[None])


def body(
    feature_pool,
    sample_ids,
    token_mask,
    step_index,
    dw_kernel,
    dw_bias,
    ln_gain,
    ln_bias,
    w_in,
    grn_gamma,
    grn_beta,
    w_out,
):
    if lax.axis_size("shard") != 2:
        return general_body(
            feature_pool, sample_ids, token_mask, step_index, dw_kernel, dw_bias,
            ln_gain, ln_bias, w_in, grn_gamma, grn_beta, w_out,
        )
    levels = lax.axis_size("gossip").bit_length() - 1
    pick = (sample_ids[0] + step_index[0] // levels) % feature_pool.shape[1]
    me = lax.axis_index("shard").astype(jnp.int32)
    outs = lax.switch(
        step_index[0] % levels,
        [partial(pair_body, bit) for bit in range(levels)],
        feature_pool[0], pick, token_mask[0], me, dw_kernel, dw_bias, ln_gain, ln_bias,
        w_in[0], grn_gamma[0], grn_beta[0], w_out[0],
    )
    return tuple(out[None] for out in outs)


def solution(mesh):
    in_specs = (
        P("gossip", None, "shard", None, None),
        P("gossip"),
        P("gossip", "shard", None),
        P(),
        P(),
        P(),
        P(),
        P(),
        P("gossip", "shard", None),
        P("gossip", "shard"),
        P("gossip", "shard"),
        P("gossip", "shard", None),
    )
    out_specs = (
        P("gossip", "shard", None),
        P("gossip", "shard", None),
        P("gossip", "shard"),
        P("gossip", "shard"),
    )
    return jax.shard_map(body, mesh=mesh, in_specs=in_specs, out_specs=out_specs, check_vma=False)
```

```python
from functools import partial
import math

import jax
import jax.numpy as jnp
from jax import lax
from jax.experimental import pallas as pl
from jax.experimental.pallas import tpu as pltpu
from jax.sharding import PartitionSpec as P

HID = 3072
H = 32
W = 32
POOL = 2
LANES = 128
F32 = jnp.float32
BF16 = jnp.bfloat16
NT = (((1,), (1,)), ((), ()))
TN = (((0,), (0,)), ((), ()))
NN = (((1,), (0,)), ((), ()))


def shape_of(dims, dtype):
    return jax.ShapeDtypeStruct(dims, dtype)


def whole(dims):
    return pl.BlockSpec(dims, lambda i: (0,) * len(dims))


def rows_at(block, width, offset=0, side=0):
    return pl.BlockSpec((block, width), lambda i: (i + offset, side))


def call(kernel, grid, in_specs, out_specs, out_shape, scratch=(), aliases=None, needed=()):
    inputs, extra = len(in_specs), len(needed)

    def run(*refs):
        kernel(*refs[:inputs], *refs[inputs + extra:])

    def placed(shape):
        return pltpu.HBM(shape.shape, shape.dtype) if math.prod(shape.shape) > 1 << 16 else shape

    single = not isinstance(out_shape, list)
    held = placed(out_shape) if single else [placed(s) for s in out_shape]
    built = pl.pallas_call(
        run,
        grid=(grid,),
        in_specs=list(in_specs) + [pl.BlockSpec(memory_space=pl.ANY)] * extra,
        out_specs=out_specs,
        out_shape=held,
        scratch_shapes=list(scratch),
        input_output_aliases=aliases or {},
        compiler_params=pltpu.CompilerParams(
            dimension_semantics=("arbitrary",), vmem_limit_bytes=48 * 1024 * 1024
        ),
    )
    def in_hbm(value):
        return pltpu.with_memory_space_constraint(value, pltpu.HBM) if value.size > 1 << 16 else value

    return lambda *args: built(*map(in_hbm, args), *map(in_hbm, needed))


def lane_tiles(width):
    return [slice(k * LANES, (k + 1) * LANES) for k in range(width // LANES)]


def folded(value):
    tiles = [value[:, t] for t in lane_tiles(value.shape[1])]
    return sum(tiles[1:], tiles[0])


def conv_kernel(me_ref, live_own_ref, live_other_ref, tap_ref, bias_ref, gain_ref, shift_ref, *refs,
                parts, out_rows, half, copies, held):
    scratch = 4 + bool(copies)
    outs = 1 + bool(copies)
    sources = refs[:len(refs) - scratch - outs - held]
    out_ref = refs[-scratch - outs]
    pad_ref, conv_ref, norm_ref, sems = refs[-scratch:len(refs) - scratch + 4]
    rows, cols, _ = live_own_ref.shape
    blocks = conv_ref.shape[0]
    window = out_rows + 6
    upper = me_ref[0] == 0
    inner = slice(8, 8 + cols)
    moves = []
    if copies:
        map_ref, map_sems = refs[-scratch - 1], refs[-1]
        for n, (source, at, mirrored) in enumerate(copies):
            there = pl.ds(jnp.where(upper, at, mirrored), sources[source].shape[0])
            moves.append(pltpu.make_async_copy(sources[source], map_ref.at[there], map_sems.at[n]))
            moves[-1].start()
    pad_ref[:, 0:8, :] = jnp.zeros((window, 8, LANES), F32)
    pad_ref[:, 8 + cols:, :] = jnp.zeros((window, 8, LANES), F32)
    group = 8

    def one_block(c, carry):
        lane = pl.ds(pl.multiple_of(c * LANES, LANES), LANES)
        for source, count, distance, place in parts:
            there = pl.ds(jnp.where(upper, place, window - count - place), count)
            if source is None:
                pad_ref[there, inner, :] = jnp.zeros((count, cols, LANES), F32)
                continue
            own = distance < 0
            live_ref = live_own_ref if own else live_other_ref
            first = jnp.where(upper, distance + rows if own else distance,
                              -distance - count if own else rows - distance - count)
            length = sources[source].shape[0]
            values = sources[source][pl.ds(jnp.where(upper, length - count, 0), count), :, lane]
            pad_ref[there, inner, :] = values.astype(F32) * live_ref[pl.ds(first, count)]

        def one_group(g, carry):
            base = g * group
            acc = [jnp.broadcast_to(bias_ref[:, lane], (cols, LANES)) for _ in range(group)]
            for j in range(7):
                for q in range(group + 6):
                    x = pad_ref[base + q, 5 + j:5 + j + cols, :]
                    for r in range(max(0, q - 6), min(group, q + 1)):
                        tap = (q - r) * 7 + j
                        acc[r] = acc[r] + x * tap_ref[tap:tap + 1, lane]
            for r in range(group):
                conv_ref[c, pl.ds((base + r) * cols, cols), :] = acc[r]
            return carry

        return lax.fori_loop(0, out_rows // group, one_group, carry, unroll=True)

    lax.fori_loop(0, blocks, one_block, 0)
    step = 32
    channels = blocks * LANES
    base = 0
    if half is not None:
        base = jnp.where(upper, half, 1 - half) * (out_rows * cols)

    def one_step(t, carry):
        here = pl.ds(pl.multiple_of(t * step, step), step)
        values = [conv_ref[k, here, :] for k in range(blocks)]
        center = jnp.sum(sum(values[1:], values[0]), axis=1, keepdims=True) / channels
        away = [v - center for v in values]
        squares = [d * d for d in away]
        spread = jnp.sum(sum(squares[1:], squares[0]), axis=1, keepdims=True) / channels
        inverse = lax.rsqrt(spread + 1e-06)
        for k, t_k in enumerate(lane_tiles(channels)):
            norm_ref[here, t_k] = (away[k] * inverse * gain_ref[:, t_k] + shift_ref[:, t_k]).astype(BF16)
        return carry

    quarter = out_rows * cols // 4
    for n in range(4):
        lax.fori_loop(n * quarter // step, (n + 1) * quarter // step, one_step, 0, unroll=True)
        there = pl.ds(pl.multiple_of(base + n * quarter, quarter), quarter)
        moves.append(pltpu.make_async_copy(norm_ref.at[n * quarter:(n + 1) * quarter], out_ref.at[there], sems.at[n]))
        moves[-1].start()
    for move in moves:
        move.wait()


def conv_norm(me, lives, maps, parts, half, vectors, copies=(), filled=(), needed=()):
    rows, cols = lives[0].shape[:2]
    channels = vectors[0].shape[1]
    blocks = channels // LANES
    out_rows = rows if half is None else rows // 2
    inputs = 7 + len(maps)
    held = len(filled)
    place = pl.BlockSpec(memory_space=pltpu.HBM)
    more = bool(copies)
    return call(
        partial(conv_kernel, parts=parts, out_rows=out_rows, half=half, copies=copies, held=held),
        1,
        [pl.BlockSpec(memory_space=pltpu.SMEM)]
        + [whole(v.shape) for v in (*lives, *vectors, *maps)]
        + [pl.BlockSpec(memory_space=pl.ANY)] * held,
        [place] * (1 + more),
        [shape_of((rows * cols, channels), BF16)] + [shape_of((rows, cols, channels), BF16)] * more,
        [
            pltpu.VMEM((out_rows + 6, cols + 16, LANES), F32),
            pltpu.VMEM((blocks, out_rows * cols, LANES), F32),
            pltpu.VMEM((out_rows * cols, channels), BF16),
            pltpu.SemaphoreType.DMA((4,)),
        ] + [pltpu.SemaphoreType.DMA((len(copies),))] * more,
        aliases={inputs: 0} if held else None,
        needed=needed,
    )(me, *lives, *vectors, *maps, *filled)


def columns_kernel(gamma_ref, beta_ref, gamma_out, beta_out):
    for row, out in ((gamma_ref, gamma_out), (beta_ref, beta_out)):
        out[...] = jnp.broadcast_to(row[...], (LANES, row.shape[1])).T


def columns(gamma, beta):
    units = gamma.shape[0]
    return call(
        columns_kernel, 1, [whole((1, units))] * 2, [whole((units, LANES))] * 2,
        [shape_of((units, LANES), F32)] * 2,
    )(gamma[None], beta[None])


def expand_block(normed_ref, w_ref, hidden_ref, slope_ref):
    pre_act = lax.dot_general(w_ref[...], normed_ref[...], NT, preferred_element_type=F32)
    cdf = 0.5 * (1.0 + lax.erf(pre_act * math.sqrt(0.5)))
    hidden = pre_act * cdf
    hidden_ref[...] = hidden.astype(BF16)
    slope = cdf + pre_act * (jnp.exp(-0.5 * pre_act * pre_act) * (1.0 / math.sqrt(2.0 * math.pi)))
    slope_ref[...] = slope.astype(BF16)
    return folded(hidden * hidden)


def expand_first_kernel(normed_ref, w_ref, hidden_ref, slope_ref, square_ref):
    square_ref[...] = expand_block(normed_ref, w_ref, hidden_ref, slope_ref)


def expand_last_kernel(normed_ref, w_ref, before_ref, _, hidden_ref, slope_ref, norms_ref, total_ref):
    square = expand_block(normed_ref, w_ref, hidden_ref, slope_ref) + before_ref[...]
    norms = jnp.sqrt(jnp.sum(square, axis=1, keepdims=True) + 1e-06)
    norms_ref[...] = jnp.broadcast_to(norms, norms_ref.shape)

    @pl.when(pl.program_id(0) == 0)
    def _():
        total_ref[...] = jnp.zeros_like(total_ref)

    total_ref[...] += jnp.sum(norms)


def expand(normed, w, before=None, filled=None):
    tokens, channels = normed.shape
    units = w.shape[0]
    block = 512
    last = before is not None
    lane = rows_at(block, LANES)
    out_specs = [rows_at(block, tokens, 0, int(last)), rows_at(block, tokens), lane] + [whole((8, LANES))] * last
    out_shape = [shape_of((units, 2 * tokens), BF16), shape_of((units, tokens), BF16), shape_of((units, LANES), F32)]
    out_shape += [shape_of((8, LANES), F32)] * last
    return call(
        expand_last_kernel if last else expand_first_kernel,
        units // block,
        [whole((tokens, channels)), rows_at(block, channels)]
        + [lane, pl.BlockSpec(memory_space=pl.ANY)] * last,
        out_specs,
        out_shape,
        aliases={3: 0} if last else None,
    )(normed, w, *([before, filled] if last else []))


def project_kernel(total_ref, peer_ref, norms_ref, gamma_ref, beta_ref, hidden_own_ref, hidden_other_ref, w_ref,
                   mixed_ref, part_own_ref, part_other_ref, scale_ref, acc_ref, *, steps, units_all):
    k = pl.program_id(0)
    divisor = (total_ref[0:1, :] + peer_ref[0:1, :]) / units_all + 1e-06
    scale = gamma_ref[...] * (norms_ref[...] / divisor) + 1.0
    shift = beta_ref[...]
    scale_ref[...] = scale
    tokens = hidden_own_ref.shape[1]
    for base, hidden_ref in ((0, hidden_own_ref), (tokens, hidden_other_ref)):
        for t in lane_tiles(tokens):
            value = hidden_ref[:, t].astype(F32) * scale + shift
            mixed_ref[:, base + t.start:base + t.stop] = value.astype(BF16)
    for n, part_ref in ((0, part_own_ref), (1, part_other_ref)):
        product = lax.dot_general(
            mixed_ref[:, n * tokens:(n + 1) * tokens], w_ref[...], TN, preferred_element_type=F32
        )

        @pl.when(k == 0)
        def _():
            acc_ref[n] = product

        @pl.when((k > 0) & (k < steps - 1))
        def _():
            acc_ref[n] += product

        @pl.when(k == steps - 1)
        def _():
            part_ref[...] = (acc_ref[n] + product).astype(BF16)


def project(total, peer, norms, gamma, beta, hidden, w, units_all, needed=()):
    units, tokens = hidden.shape[0], hidden.shape[1] // 2
    channels = w.shape[1]
    block = 512
    lane, tiny, part = rows_at(block, LANES), whole((8, LANES)), whole((tokens, channels))
    return call(
        partial(project_kernel, steps=units // block, units_all=units_all),
        units // block,
        [tiny, tiny, lane, lane, lane, rows_at(block, tokens), rows_at(block, tokens, 0, 1), rows_at(block, channels)],
        [rows_at(block, 2 * tokens), part, part, lane],
        [shape_of((units, 2 * tokens), BF16)] + [shape_of((tokens, channels), BF16)] * 2
        + [shape_of((units, LANES), F32)],
        [pltpu.VMEM((2, tokens, channels), F32)],
        needed=needed,
    )(total, peer, norms, gamma, beta, hidden, hidden, w)


def back_block(part_ref, peer_ref, target_ref, live_ref, w_ref, hidden_ref, errors_ref, back_ref, scale):
    @pl.when(pl.program_id(0) == 0)
    def _():
        live = live_ref[...]
        keep = (1.0 - live) * scale
        for t in lane_tiles(target_ref.shape[1]):
            target = target_ref[:, t].astype(F32)
            summed = part_ref[:, t].astype(F32) + peer_ref[:, t].astype(F32)
            errors_ref[:, t] = (keep * (target * live + summed - target)).astype(BF16)

    back = lax.dot_general(w_ref[...], errors_ref[...], NT, preferred_element_type=F32)
    back_ref[...] = back.astype(BF16)
    return folded(back), folded(back * hidden_ref[...].astype(F32))


def back_first_kernel(part_ref, peer_ref, target_ref, live_ref, w_ref, hidden_ref,
                      errors_ref, back_ref, sum_ref, dot_ref, *, scale):
    sum_ref[...], dot_ref[...] = back_block(
        part_ref, peer_ref, target_ref, live_ref, w_ref, hidden_ref, errors_ref, back_ref, scale
    )


def back_last_kernel(part_ref, peer_ref, target_ref, live_ref, w_ref, hidden_ref,
                     sum_before_ref, dot_before_ref, total_ref, peer_total_ref, norms_ref, gamma_ref,
                     errors_ref, back_ref, beta_out_ref, gamma_out_ref, dots_ref, slope_ref, *, scale, units_all):
    sums, dots = back_block(
        part_ref, peer_ref, target_ref, live_ref, w_ref, hidden_ref, errors_ref, back_ref, scale
    )
    lanes = beta_out_ref.shape
    sums = jnp.sum(sums + sum_before_ref[...], axis=1, keepdims=True)
    dots = jnp.broadcast_to(jnp.sum(dots + dot_before_ref[...], axis=1, keepdims=True), lanes)
    divisor = (total_ref[0:1, :] + peer_total_ref[0:1, :]) / units_all + 1e-06
    norms = norms_ref[...]
    beta_out_ref[...] = jnp.broadcast_to(sums, lanes)
    gamma_out_ref[...] = dots * (norms / divisor)
    dots_ref[...] = dots
    slopes = dots * gamma_ref[...] * (-norms / (divisor * divisor * units_all))

    @pl.when(pl.program_id(0) == 0)
    def _():
        slope_ref[...] = jnp.zeros_like(slope_ref)

    slope_ref[...] += jnp.sum(slopes[:, 0:1])


def back_pass(part, peer, target, live, w, hidden, side, scale, units_all, more=None, needed=()):
    tokens, channels = part.shape
    units = w.shape[0]
    block = 768
    lane, tiny, full = rows_at(block, LANES), whole((8, LANES)), whole((tokens, channels))
    in_specs = [full, full, full, whole((tokens, LANES)), rows_at(block, channels), rows_at(block, tokens, 0, side)]
    out_specs = [full, rows_at(block, tokens), lane, lane]
    out_shape = [shape_of((tokens, channels), BF16), shape_of((units, tokens), BF16)]
    out_shape += [shape_of((units, LANES), F32)] * 2
    kernel = partial(back_first_kernel, scale=scale)
    if more is not None:
        kernel = partial(back_last_kernel, scale=scale, units_all=units_all)
        in_specs += [lane, lane, tiny, tiny, lane, lane]
        out_specs += [lane, tiny]
        out_shape += [shape_of((units, LANES), F32), shape_of((8, LANES), F32)]
    return call(
        kernel, units // block, in_specs, out_specs, out_shape, needed=needed,
    )(part, peer, target, live, w, hidden, *(more or ()))


def pre_grad_kernel(total_ref, peer_ref, slope_ref, peer_slope_ref, norms_ref, gamma_ref, dots_ref,
                    back_a, back_b, hidden_a, hidden_b, bend_a, bend_b, out_ref, *, units_all):
    divisor = (total_ref[0:1, :] + peer_ref[0:1, :]) / units_all + 1e-06
    d_total = slope_ref[0:1, :] + peer_slope_ref[0:1, :]
    norms = norms_ref[...]
    gamma = gamma_ref[...]
    ratio = norms / divisor
    along = gamma * ratio + 1.0
    across = (gamma * dots_ref[...] / divisor + d_total) / norms
    tokens = back_a.shape[1]
    for base, back, hidden, bend in ((0, back_a, hidden_a, bend_a), (tokens, back_b, hidden_b, bend_b)):
        for t in lane_tiles(tokens):
            value = (back[:, t].astype(F32) * along + across * hidden[:, t].astype(F32)) * bend[:, t].astype(F32)
            out_ref[:, base + t.start:base + t.stop] = value.astype(BF16)


def pre_grad(first, count, total, peer, slope, peer_slope, norms, gamma, dots, backs, hidden, bends, units_all,
             needed=()):
    tokens = backs[0].shape[1]
    block = 256
    at = first // block
    lane, tiny, wide = rows_at(block, LANES, at), whole((8, LANES)), rows_at(block, tokens, at)
    return call(
        partial(pre_grad_kernel, units_all=units_all),
        count // block,
        [tiny] * 4 + [lane] * 3 + [wide] * 2 + [wide, rows_at(block, tokens, at, 1)] + [wide] * 2,
        rows_at(block, 2 * tokens),
        shape_of((count, 2 * tokens), BF16),
        needed=needed,
    )(total, peer, slope, peer_slope, norms, gamma, dots, *backs, hidden, hidden, *bends)


def pair_kernel(*refs, terms, carried, final, scaled):
    out_ref = refs[-1]
    after_terms = 2 * terms + carried
    total = refs[2 * terms][...] if carried else None
    for n in range(terms):
        left = refs[n][...]
        if n in scaled:
            scale, shift = refs[after_terms][:, 0:1], refs[after_terms + 1][:, 0:1]
            left = (left.astype(F32) * scale + shift).astype(BF16)
        product = lax.dot_general(left, refs[terms + n][...], NN, preferred_element_type=F32)
        total = product if total is None else total + product
    out_ref[...] = (total * 0.5).astype(BF16) if final else total


def pair_sum(terms, first=0, units=None, carried=None, final=True, filled=None, needed=(), scaled=(), scales=()):
    count = terms[0][0].shape[0]
    tokens, channels = terms[0][2].shape
    units = units or count
    block = 256
    sums = [] if carried is None else [carried]
    held = [] if filled is None else [filled]
    inputs = 2 * len(terms) + len(sums) + len(scales)
    return call(
        partial(pair_kernel, terms=len(terms), carried=bool(sums), final=final, scaled=scaled),
        count // block,
        [rows_at(block, tokens, 0, half) for _, half, _ in terms] + [whole((tokens, channels))] * len(terms)
        + [rows_at(block, channels)] * len(sums)
        + [rows_at(block, LANES)] * len(scales)
        + [pl.BlockSpec(memory_space=pl.ANY)] * len(held),
        rows_at(block, channels, first // block),
        shape_of((units, channels), BF16 if final else F32),
        aliases={inputs: 0} if held else None,
        needed=needed,
    )(*[t[0] for t in terms], *[t[2] for t in terms], *sums, *scales, *held)


def after(value, *needed):
    place = pl.BlockSpec(memory_space=pl.ANY)
    return pl.pallas_call(
        lambda *refs: None,
        in_specs=[place] * (1 + len(needed)),
        out_specs=place,
        out_shape=shape_of(value.shape, value.dtype),
        input_output_aliases={0: 0},
    )(value, *needed)


def pair_body(bit, pool, pick, token_mask, me, dw_kernel, dw_bias, ln_gain, ln_bias, w_in, grn_gamma, grn_beta, w_out):
    _, rows, cols, channels = pool.shape
    units = w_in.shape[0]
    units_all = 2 * units
    tokens = rows * cols
    scale = 1.0 / math.sqrt(2 * tokens)
    direct = bit == 0
    shared = bit >= 3

    def across(value):
        return lax.ppermute(value, "shard", [(0, 1), (1, 0)])

    def to_peer(value):
        return lax.ppermute(value, "gossip", [(i, i ^ 1 << bit) for i in range(lax.axis_size("gossip"))])

    def live_of(keep):
        return jnp.broadcast_to((1.0 - keep.astype(F32))[..., None], (rows, cols, LANES))

    def cut(start, count):
        return lax.dynamic_slice(pool, (pick, start, 0, 0), (1, count, cols, channels))[0]

    near, far = rows // 2, rows - rows // 2 - 3
    upper = me == 0
    edge = cut(jnp.where(upper, rows - 3, 0), 3)
    edge_other = across(edge)
    mask_other = across(token_mask)
    sample = cut(0, rows)
    taps = dw_kernel.reshape(49, channels)
    mid_other = across(after(cut(jnp.where(upper, far, 3), near), edge_other, mask_other, sample, taps))
    far_other = across(cut(jnp.where(upper, 0, 3 + near), far))
    live, live_other = live_of(token_mask), live_of(mask_other)
    vectors = [taps] + [v.reshape(1, channels) for v in (dw_bias, ln_gain, ln_bias)]
    gamma, beta = columns(grn_gamma, grn_beta)
    me_vec = me.reshape(1)

    normed_own, = conv_norm(
        me_vec, (live, live_other), (sample, edge_other),
        ((None, 3, 0, 0), (0, rows, -rows, 3), (1, 3, 0, rows + 3)), None, vectors,
    )
    normed_other, = conv_norm(
        me_vec, (live, live_other), (edge, edge_other, mid_other),
        ((0, 3, -3, 0), (1, 3, 0, 3), (2, near, 3, 6)), 0, vectors, needed=(normed_own,),
    )
    normed_own = after(normed_own, normed_other)
    normed_own_p = to_peer(normed_own)
    hidden, bend_own, squares = expand(normed_own, w_in)
    normed_other, sample_other = conv_norm(
        me_vec, (live, live_other), (mid_other, far_other, edge_other),
        ((0, 6, 5, 0), (1, far, near + 3, 6), (None, 3, 0, far + 6)), 1, vectors,
        ((2, 0, rows - 3), (0, 3, far), (1, near + 3, 0)), (normed_other,), needed=(squares,),
    )
    hidden, bend_other, norms, total = expand(normed_other, w_in, squares, hidden)
    if shared:
        left_p = to_peer(hidden)
    total_x = across(total)

    mixed, part_own, part_other, scales = project(
        total, total_x, norms, gamma, beta, hidden, w_out, units_all, needed=(normed_own_p,)
    )
    came_own = across(part_other)
    scales_p = ()
    if shared:
        scales_p = to_peer(jnp.stack([scales[:, 0], grn_beta]))
    else:
        left_p = to_peer(mixed)
    came_other = across(part_own)

    errors_own, back_own, sums, dots = back_pass(
        part_own, came_own, sample.reshape(tokens, channels), live.reshape(tokens, LANES),
        w_out, hidden, 0, scale, units_all,
    )
    errors_own_p = to_peer(errors_own)
    errors_other, back_other, g_beta, g_gamma, dots, slope = back_pass(
        part_other, came_other, sample_other.reshape(tokens, channels), live_other.reshape(tokens, LANES),
        w_out, hidden, 1, scale, units_all, (sums, dots, total, total_x, norms, gamma),
    )
    small = jnp.stack([g_gamma[:, 0], g_beta[:, 0]])
    slope_x = across(slope)
    if direct:
        normed_other_p = to_peer(normed_other)
        errors_other_p = to_peer(errors_other)
        counts = (units,)
    else:
        normed_own_p = after(normed_own_p, slope_x)
        normed_other_p = across(normed_own_p)
        counts = (units // 2, units // 3, units // 6)
    small_p = to_peer(small)
    if shared:
        scales_p = columns(scales_p[0], scales_p[1])

    pieces, sums = [], []
    first = 0
    for n, count in enumerate(counts):
        own = pre_grad(
            first, count, total, total_x, slope, slope_x, norms, gamma, dots,
            (back_own, back_other), hidden, (bend_own, bend_other), units_all,
            needed=tuple(own for _, own, _ in pieces[-1:]) + ((normed_own_p,) if n == 0 and shared else ()) + ((left_p, *scales_p) if n == 1 else ()) + ((normed_other_p,) if n == 2 else ()),
        )
        pieces.append((first, own, to_peer(own)))
        if not direct:
            sums.append(pair_sum(((own, 0, normed_own), (own, 1, normed_other)), final=False))
        first += count
        if not direct and n == 1:
            errors_own_p = after(errors_own_p, own, *sums)
            errors_other_p = across(errors_own_p)
            early = pair_sum(
                ((mixed, 0, errors_own), (left_p, 0, errors_own_p)), final=False, scaled=(1,) if shared else (), scales=scales_p
            )
    out_terms = ((mixed, 1, errors_other), (left_p, 1, errors_other_p))
    if direct:
        out_terms += ((mixed, 0, errors_own), (left_p, 0, errors_own_p))
    grad_out = pair_sum(out_terms, carried=None if direct else early, scaled=(1,) if shared else (), scales=scales_p)
    grad_in = None
    for n, (first, own, peer) in enumerate(pieces):
        own_terms = ((own, 0, normed_own), (own, 1, normed_other))
        peer_terms = ((peer, 0, normed_own_p), (peer, 1, normed_other_p))
        gate = (grad_out,) if n == (0 if direct else 1) else ()
        if direct:
            grad_in = pair_sum(own_terms + peer_terms, first, units, None, True, grad_in, gate)
            continue
        if n == 0:
            gate = (early, *sums[1:])
        grad_in = pair_sum(peer_terms, first, units, sums[n], True, grad_in, gate)
        if n == 1:
            small_p = after(small_p, grad_in)
    small = (small + small_p) * 0.5
    return grad_in, grad_out, small[0], small[1]


def shortened(value):

    def short(part):
        return part.astype(jnp.bfloat16) if part.dtype == jnp.float32 else part

    return jax.tree.map(short, value)


def from_partner(value, axis, distance):
    return lax.ppermute(value, axis, [(i, i ^ 1 << distance) for i in range(lax.axis_size(axis))])


def with_halo(block, sides, width):
    for axis, dim in sides:
        count = lax.axis_size(axis)
        forward = [(i, i + 1) for i in range(count - 1)]
        backward = [(target, source) for source, target in forward]
        low = lax.ppermute(
            lax.slice_in_dim(block, block.shape[dim] - width, None, axis=dim), axis, forward
        )
        high = lax.ppermute(lax.slice_in_dim(block, 0, width, axis=dim), axis, backward)
        block = jnp.concatenate([low, block, high], axis=dim)
    return block


def depthwise(padded, kernel, bias_vec, height_rows, width_cols):
    result = jnp.zeros((height_rows, width_cols, kernel.shape[2]), jnp.float32)
    for i in range(7):
        for j in range(7):
            result = (
                result
                + padded[i : i + height_rows, j : j + width_cols].astype(jnp.float32) * kernel[i, j]
            )
    return result + bias_vec


def normalize(values, gain_vec, shift_vec):
    center = jnp.mean(values, axis=-1, keepdims=True)
    spread = jnp.mean(jnp.square(values - center), axis=-1, keepdims=True)
    return (values - center) * lax.rsqrt(spread + 1e-06) * gain_vec + shift_vec


def gelu_slope(pre_act):
    cdf_part = 0.5 * (1.0 + lax.erf(pre_act / math.sqrt(2.0)))
    pdf_part = jnp.exp(-0.5 * pre_act * pre_act) / math.sqrt(2.0 * math.pi)
    return cdf_part + pre_act * pdf_part


def peer_swap(payload, which_bit):
    return jax.tree.map(
        lambda part, own: part.astype(own.dtype),
        from_partner(shortened(payload), "gossip", which_bit),
        payload,
    )


def general_body(
    feature_pool,
    sample_ids,
    token_mask,
    step_index,
    dw_kernel,
    dw_bias,
    ln_gain,
    ln_bias,
    w_in,
    grn_gamma,
    grn_beta,
    w_out,
):
    levels = lax.axis_size("gossip").bit_length() - 1
    rotation = step_index[0] // levels
    pick = (sample_ids[0] + rotation) % POOL
    sample = lax.dynamic_index_in_dim(feature_pool[0], pick, 0, keepdims=False)
    keep = token_mask[0]
    local_rows, width_cols, channels = sample.shape
    w_in_local = w_in[0]
    w_out_local = w_out[0]
    gamma_vec = grn_gamma[0]
    beta_vec = grn_beta[0]
    error_scale = 1.0 / math.sqrt(H * W)
    masked = (sample.astype(jnp.float32) * (1.0 - keep.astype(jnp.float32))[..., None]).astype(
        jnp.bfloat16
    )
    rimmed = with_halo(masked, (("shard", 0),), 3)
    padded = jnp.pad(rimmed, ((0, 0), (3, 3), (0, 0)))
    normed = (
        normalize(depthwise(padded, dw_kernel, dw_bias, local_rows, width_cols), ln_gain, ln_bias)
        .astype(jnp.bfloat16)
        .reshape(-1, channels)
    )
    gathered = lax.all_gather(normed, "shard", axis=0, tiled=True)
    pre_act = lax.dot_general(
        gathered, w_in_local, (((1,), (1,)), ((), ())), preferred_element_type=jnp.float32
    )
    hidden = jax.nn.gelu(pre_act, approximate=False)
    norms = jnp.sqrt(jnp.sum(hidden * hidden, axis=0) + 1e-06)
    norm_total = lax.psum(jnp.sum(norms), "shard")
    divisor = norm_total / HID + 1e-06
    ratio = norms / divisor
    mixed = (gamma_vec * (hidden * ratio) + beta_vec + hidden).astype(jnp.bfloat16)
    own_sum = lax.psum_scatter(
        jnp.dot(mixed, w_out_local, preferred_element_type=jnp.float32).astype(jnp.bfloat16),
        "shard",
        scatter_dimension=0,
        tiled=True,
    ).astype(jnp.float32)
    output_own = masked.astype(jnp.float32).reshape(-1, channels) + own_sum
    target_own = sample.astype(jnp.float32).reshape(-1, channels)
    errors_own = (
        keep.astype(jnp.float32).reshape(-1, 1) * (output_own - target_own) * error_scale
    ).astype(jnp.bfloat16)
    errors_all = lax.all_gather(errors_own, "shard", axis=0, tiled=True)
    grad_out_local = lax.dot_general(
        mixed, errors_all, (((0,), (0,)), ((), ())), preferred_element_type=jnp.float32
    )
    back = lax.dot_general(
        errors_all, w_out_local, (((1,), (1,)), ((), ())), preferred_element_type=jnp.float32
    )
    grad_gamma_local = jnp.sum(back * hidden * ratio, axis=0)
    grad_beta_local = jnp.sum(back, axis=0)
    d_ratio = jnp.sum(back * gamma_vec * hidden, axis=0)
    slope_local = jnp.sum(d_ratio * (-norms / (divisor * divisor * HID)))
    d_total = lax.psum(slope_local, "shard")
    d_norms = d_ratio / divisor + d_total
    d_hidden = back * (gamma_vec * ratio + 1.0) + d_norms / norms * hidden
    d_pre = (d_hidden * gelu_slope(pre_act)).astype(jnp.bfloat16)
    grad_in_local = lax.dot_general(
        d_pre, gathered, (((0,), (0,)), ((), ())), preferred_element_type=jnp.float32
    )
    own_grads = (grad_in_local, grad_out_local, grad_gamma_local, grad_beta_local)
    branches = [partial(peer_swap, which_bit=b) for b in range(levels)]
    peer_grads = lax.switch(step_index[0] % levels, branches, own_grads)
    grad_in = ((own_grads[0] + peer_grads[0]) * 0.5).astype(jnp.bfloat16)
    grad_out = ((own_grads[1] + peer_grads[1]) * 0.5).astype(jnp.bfloat16)
    grad_gamma = (own_grads[2] + peer_grads[2]) * 0.5
    grad_beta = (own_grads[3] + peer_grads[3]) * 0.5
    return (grad_in[None], grad_out[None], grad_gamma[None], grad_beta[None])


def body(
    feature_pool,
    sample_ids,
    token_mask,
    step_index,
    dw_kernel,
    dw_bias,
    ln_gain,
    ln_bias,
    w_in,
    grn_gamma,
    grn_beta,
    w_out,
):
    if lax.axis_size("shard") != 2:
        return general_body(
            feature_pool, sample_ids, token_mask, step_index, dw_kernel, dw_bias,
            ln_gain, ln_bias, w_in, grn_gamma, grn_beta, w_out,
        )
    levels = lax.axis_size("gossip").bit_length() - 1
    pick = (sample_ids[0] + step_index[0] // levels) % feature_pool.shape[1]
    me = lax.axis_index("shard").astype(jnp.int32)
    outs = lax.switch(
        step_index[0] % levels,
        [partial(pair_body, bit) for bit in range(levels)],
        feature_pool[0], pick, token_mask[0], me, dw_kernel, dw_bias, ln_gain, ln_bias,
        w_in[0], grn_gamma[0], grn_beta[0], w_out[0],
    )
    return tuple(out[None] for out in outs)


def solution(mesh):
    in_specs = (
        P("gossip", None, "shard", None, None),
        P("gossip"),
        P("gossip", "shard", None),
        P(),
        P(),
        P(),
        P(),
        P(),
        P("gossip", "shard", None),
        P("gossip", "shard"),
        P("gossip", "shard"),
        P("gossip", "shard", None),
    )
    out_specs = (
        P("gossip", "shard", None),
        P("gossip", "shard", None),
        P("gossip", "shard"),
        P("gossip", "shard"),
    )
    return jax.shard_map(body, mesh=mesh, in_specs=in_specs, out_specs=out_specs, check_vma=False)
```
